32 devices in a mesh: dp: 4 (over y, x), seq: 8 (over z, core).
Axes of the slice: x: 2, y: 2, z: 4, core: 2. Of those that a mesh axis runs over, the one named last changes fastest.
Arguments:
- queries: bfloat16 [4, 1024, 2048], P('dp', 'seq'), may hold values from -6 to 6
- attended_grad: bfloat16 [4, 1024, 2048], P('dp', 'seq'), may hold values from -6 to 6
- neighbour_pool: bfloat16 [4, 32, 128, 896], P('dp', 'seq'), may hold values from -6 to 6
- stretch_slot: int32 [4, 16], P('dp'), may hold values from 0 to 31, as said below
- enc_gain: float32 [896], replicated, may hold values from 0.1 to 1.9
- enc_up: bfloat16 [896, 1792], replicated, may hold values from -0.1875 to 0.1875
- enc_down: bfloat16 [1792, 896], replicated, may hold values from -0.125 to 0.125
- key_weight: bfloat16 [896, 2048], P(None, 'seq'), may hold values from -0.1875 to 0.1875
- value_weight: bfloat16 [896, 2048], P(None, 'seq'), may hold values from -0.1875 to 0.1875
Outputs:
- attended: bfloat16 [4, 1024, 2048], P('dp', 'seq')
- query_grad: bfloat16 [4, 1024, 2048], P('dp', 'seq')
- pool_grad: bfloat16 [4, 32, 128, 896], P('dp', 'seq')
- key_weight_grad: float32 [896, 2048], P(None, 'seq')
- value_weight_grad: float32 [896, 2048], P(None, 'seq')
The draws below stay inside these ranges and needn't reach their ends.
Inputs may be any that keep to these rules, and one draw needn't show every extreme that they name: `stretch_slot`: slot s is held by the device s // 4 along seq. No slot is named twice within a sequence, and in every sequence some device holds 4 named slots.
All inputs are finite; a program needn't handle non-finite values.
Results may differ from the reference program's by a relative error of at most 0.03.
Values may be sent and summed in bfloat16 or wider, within the bound.
No kernel may reach another device: no remote copies, remote signals or barrier semaphores. Data moves between devices by JAX's collectives and lax.ppermute only.
A program may use at most 128 MiB of HBM per device.

```python
import math
import jax
import jax.numpy as jnp
from jax import lax

STRETCHES_DEV = 2
STRETCH = 64
NLEN = 128
DE = 896
FFE = 1792
HEADS = 16
HD = 128
HQ = 2048
CAP = 4
SLOTS = 32
STRETCHES = 16
L = 1024
SEQS = 4
N_SEQ = 8


def draw_stretch_slot(key, part):
    key = jax.random.fold_in(key, 11)

    def one_sequence(seq_key):
        busy_key, order_key, shuffle_key = jax.random.split(seq_key, 3)
        busiest = jax.random.randint(busy_key, (), 0, SLOTS // CAP)
        order = jax.random.permutation(order_key, SLOTS).astype(jnp.int32)
        slot_rank = jnp.zeros((SLOTS,), jnp.int32).at[order].set(jnp.arange(SLOTS, dtype=jnp.int32))
        elsewhere = (jnp.arange(SLOTS, dtype=jnp.int32) // CAP != busiest).astype(jnp.int32)
        priority = elsewhere * SLOTS + slot_rank
        chosen = jnp.argsort(priority, stable=True)[:STRETCHES].astype(jnp.int32)
        return jax.random.permutation(shuffle_key, chosen).astype(jnp.int32)
    return jax.vmap(one_sequence)(jax.random.split(key, SEQS))


def shard_levels(own_key, dims, cuts, low, high):
    loudness, own = 1.0, jax.random.fold_in(own_key, 6)
    for dim, shards_of in cuts:
        steps = jnp.exp(jax.random.uniform(jax.random.fold_in(own, dim), (shards_of,), jnp.float32, low / len(cuts), high / len(cuts)))
        loudness = loudness * jnp.repeat(steps, dims[dim] // shards_of).reshape([-1 if axis == dim else 1 for axis in range(len(dims))])
    return loudness


def normal_values(own_key, dims, spread, bound, pieces=(), kind=jnp.bfloat16):
    values = jax.random.normal(own_key, dims, jnp.float32) * spread
    if len(pieces) > 0:
        values = shard_levels(own_key, dims, pieces, -0.22, 0.18) * values
    return jnp.clip(values, min=-bound, max=bound).astype(kind)


def setup_inputs(seed: int = 0) -> dict:
    seeds = jax.random.split(jax.random.key(seed), 10)
    return {
        "queries": normal_values(seeds[0], (SEQS, L, HQ), 1.0, 6.0, ((0, 4), (1, 8))),
        "attended_grad": normal_values(seeds[1], (SEQS, L, HQ), 1.0, 6.0, ((0, 4), (1, 8))),
        "neighbour_pool": normal_values(seeds[2], (SEQS, SLOTS, NLEN, DE), 1.0, 6.0, ((0, 4), (1, 8))),
        "stretch_slot": draw_stretch_slot(jax.random.fold_in(seeds[9], 71), 0),
        "enc_gain": jnp.clip(1.0 + 0.18 * jax.random.normal(seeds[4], (DE,), jnp.float32), 0.1, 1.9),
        "enc_up": normal_values(seeds[5], (DE, FFE), DE ** -0.5, 0.1875),
        "enc_down": normal_values(seeds[6], (FFE, DE), FFE ** -0.5, 0.125),
        "key_weight": normal_values(seeds[7], (DE, HQ), DE ** -0.5, 0.1875, ((1, 8),)),
        "value_weight": normal_values(seeds[8], (DE, HQ), DE ** -0.5, 0.1875, ((1, 8),)),
    }


epsilon = 1e-06

def encode_rows(row_block, gain_vector, up_matrix, down_matrix):
    row_values = row_block.astype(jnp.float32)
    inverse = lax.rsqrt(lax.optimization_barrier(jnp.mean(row_values * row_values, axis=-1, keepdims=True)) + epsilon)
    normed = (row_values * inverse * gain_vector).astype(jnp.bfloat16)
    before = jnp.dot(normed, up_matrix, preferred_element_type=jnp.float32)
    activity = jax.nn.gelu(before).astype(jnp.bfloat16)
    encoded = (row_values + jnp.dot(activity, down_matrix, preferred_element_type=jnp.float32)).astype(jnp.bfloat16)
    return (encoded, before, inverse)

def encode_backward(encoded_grad, row_block, before, inverse, gain_vector, up_matrix, down_matrix):
    activity_grad = jnp.dot(encoded_grad, down_matrix.T, preferred_element_type=jnp.float32)
    unused_value, gelu_back = jax.vjp(jax.nn.gelu, before)
    before_grad = gelu_back(activity_grad)[0].astype(jnp.bfloat16)
    normed_grad = jnp.dot(before_grad, up_matrix.T, preferred_element_type=jnp.float32)
    row_values = row_block.astype(jnp.float32)
    scaled_grad = gain_vector * normed_grad
    cubed = inverse * inverse * inverse
    result = encoded_grad.astype(jnp.float32) + inverse * scaled_grad - row_values * cubed * lax.optimization_barrier(jnp.mean(row_values * scaled_grad, axis=-1, keepdims=True))
    return result.astype(jnp.bfloat16)

def sequence_terms(query_seq, grad_seq, pool_seq, slot_seq, enc_gain, enc_up, enc_down, key_weight, value_weight):
    score_scale = 1.0 / math.sqrt(HD)
    used_rows = pool_seq[slot_seq.astype(jnp.int32)].reshape(STRETCHES * NLEN, DE)
    encoded_rows, before, inverse = encode_rows(used_rows, enc_gain, enc_up, enc_down)
    key_rows = jnp.dot(encoded_rows, key_weight, preferred_element_type=jnp.float32).astype(jnp.bfloat16)
    value_rows = jnp.dot(encoded_rows, value_weight, preferred_element_type=jnp.float32).astype(jnp.bfloat16)
    query_blocks = query_seq.reshape(STRETCHES, STRETCH, HEADS, HD).astype(jnp.float32)
    key_blocks = key_rows.reshape(STRETCHES, NLEN, HEADS, HD).astype(jnp.float32)
    value_blocks = value_rows.reshape(STRETCHES, NLEN, HEADS, HD).astype(jnp.float32)
    grad_blocks = grad_seq.reshape(STRETCHES, STRETCH, HEADS, HD).astype(jnp.float32)
    scores = jnp.einsum('cqhe,ckhe->chqk', query_blocks, key_blocks) * score_scale
    exponent = jnp.exp(scores)
    weights = exponent / lax.optimization_barrier(jnp.sum(exponent, axis=-1, keepdims=True))
    probabilities = weights.astype(jnp.bfloat16)
    attended = jnp.einsum('chqk,ckhe->cqhe', probabilities.astype(jnp.float32), value_blocks).astype(jnp.bfloat16).reshape(L, HQ)
    prob_grad = jnp.einsum('cqhe,ckhe->chqk', grad_blocks, value_blocks)
    score_grad = (weights * (prob_grad - lax.optimization_barrier(jnp.sum(weights * prob_grad, axis=-1, keepdims=True))) * score_scale).astype(jnp.bfloat16)
    query_grad = jnp.einsum('chqk,ckhe->cqhe', score_grad.astype(jnp.float32), key_blocks).astype(jnp.bfloat16).reshape(L, HQ)
    key_grad = jnp.einsum('chqk,cqhe->ckhe', score_grad.astype(jnp.float32), query_blocks).astype(jnp.bfloat16).reshape(STRETCHES * NLEN, HQ)
    value_grad = jnp.einsum('chqk,cqhe->ckhe', probabilities.astype(jnp.float32), grad_blocks).astype(jnp.bfloat16).reshape(STRETCHES * NLEN, HQ)
    group_rows = encoded_rows.reshape(N_SEQ, STRETCHES_DEV * NLEN, DE).astype(jnp.float32)
    key_part = jnp.einsum('nrd,nrh->ndh', group_rows, key_grad.reshape(N_SEQ, STRETCHES_DEV * NLEN, HQ).astype(jnp.float32))
    value_part = jnp.einsum('nrd,nrh->ndh', group_rows, value_grad.reshape(N_SEQ, STRETCHES_DEV * NLEN, HQ).astype(jnp.float32))
    key_total = lax.optimization_barrier(jnp.sum(lax.optimization_barrier(key_part.astype(jnp.bfloat16)).astype(jnp.float32), axis=0))
    value_total = lax.optimization_barrier(jnp.sum(lax.optimization_barrier(value_part.astype(jnp.bfloat16)).astype(jnp.float32), axis=0))
    encoded_grad = (jnp.dot(key_grad, key_weight.T, preferred_element_type=jnp.float32) + jnp.dot(value_grad, value_weight.T, preferred_element_type=jnp.float32)).astype(jnp.bfloat16)
    row_grad = encode_backward(encoded_grad, used_rows, before, inverse, enc_gain, enc_up, enc_down).reshape(STRETCHES, NLEN, DE)
    pool_grad = jnp.zeros((SLOTS, NLEN, DE), jnp.bfloat16).at[slot_seq.astype(jnp.int32)].set(row_grad)
    return (attended, query_grad, pool_grad, key_total, value_total)

def reference(queries, attended_grad, neighbour_pool, stretch_slot, enc_gain, enc_up, enc_down, key_weight, value_weight):

    def one_sequence(operands):
        return sequence_terms(operands[0], operands[1], operands[2], operands[3], enc_gain, enc_up, enc_down, key_weight, value_weight)
    attended, query_grad, pool_grad, key_totals, value_totals = lax.map(one_sequence, (queries, attended_grad, neighbour_pool, stretch_slot))
    return (attended, query_grad, pool_grad, lax.optimization_barrier(jnp.sum(key_totals, axis=0)), lax.optimization_barrier(jnp.sum(value_totals, axis=0)))
```

```python
import functools
import math

import jax
import jax.numpy as jnp
from jax import lax
from jax.experimental import pallas as pl
from jax.experimental.pallas import tpu as pltpu
from jax.sharding import Mesh, PartitionSpec as P

STRETCH = 64
HD = 128
EPSILON = 1e-06
GELU_RATE = math.sqrt(2.0 / math.pi)
GELU_CUBE = 0.044715
VMEM_BYTES = 28 * 1024 * 1024
SMALL_VMEM_BYTES = 12 * 1024 * 1024
SEQ = ("z", "core")


def dot(left, right):
    return jnp.dot(left, right, preferred_element_type=jnp.float32)


def dot_nt(left, right):
    return lax.dot_general(left, right, (((1,), (1,)), ((), ())), preferred_element_type=jnp.float32)


def dot_tn(left, right):
    return lax.dot_general(left, right, (((0,), (0,)), ((), ())), preferred_element_type=jnp.float32)


def stated(microseconds):
    return pl.CostEstimate(
        flops=microseconds * 1_000_000_000, bytes_accessed=microseconds * 3_000_000, transcendentals=0
    )


def in_hbm(value):
    return pltpu.with_memory_space_constraint(value, pltpu.HBM)


def merge_rows(block):
    pieces, rows, width = block.shape
    if rows % 16 == 0:
        return block.reshape(pieces * rows, width)
    return block.astype(jnp.float32).reshape(pieces * rows, width).astype(jnp.bfloat16)


def inverse_of(row_values):
    return lax.rsqrt(jnp.mean(row_values * row_values, axis=-1, keepdims=True) + EPSILON)


def encode_kernel(slots, rows_ref, gain_ref, up_ref, down_ref, *refs):
    enc_ref, used_ref, slope_ref, normed, total = refs[-5:]
    step = pl.program_id(0)
    count, piece, width = used_ref.shape

    @pl.when(step == 0)
    def _():
        for g in range(count):
            used_ref[g] = rows_ref[slots[g]]
        row_values = used_ref[...].astype(jnp.float32).reshape(count * piece, width)
        normed[...] = (row_values * inverse_of(row_values) * gain_ref[...]).astype(jnp.bfloat16)
        total[...] = row_values

    before = dot(normed[...], up_ref[...])
    square = before * before
    bend = jnp.tanh(GELU_RATE * before * (1.0 + GELU_CUBE * square))
    half = 0.5 * (1.0 + bend)
    activity = (before * half).astype(jnp.bfloat16)
    slope = half + 0.5 * before * (1.0 - bend * bend) * (
        GELU_RATE * (1.0 + 3.0 * GELU_CUBE * square)
    )
    slope_ref[...] = slope.astype(slope_ref.dtype)
    total[...] += dot(activity, down_ref[...])

    @pl.when(step == pl.num_programs(0) - 1)
    def _():
        enc_ref[...] = total[...].reshape(count, piece, width).astype(jnp.bfloat16)


def encode_rows(slots, rows, gain, up, down, after):
    count = slots.shape[0]
    piece, width = rows.shape[1:]
    hidden = up.shape[1]
    chunk = hidden // 2
    whole = lambda *shape: pl.BlockSpec(shape, lambda f, s: (0,) * len(shape))
    return pl.pallas_call(
        encode_kernel,
        grid_spec=pltpu.PrefetchScalarGridSpec(
            num_scalar_prefetch=1,
            grid=(hidden // chunk,),
            in_specs=[
                whole(*rows.shape),
                whole(1, width),
                pl.BlockSpec((width, chunk), lambda f, s: (0, f)),
                pl.BlockSpec((chunk, width), lambda f, s: (f, 0)),
            ]
            + [pl.BlockSpec(memory_space=pl.ANY)] * len(after),
            out_specs=[
                whole(count, piece, width),
                whole(count, piece, width),
                pl.BlockSpec((count * piece, chunk), lambda f, s: (0, f)),
            ],
            scratch_shapes=[
                pltpu.VMEM((count * piece, width), jnp.bfloat16),
                pltpu.VMEM((count * piece, width), jnp.float32),
            ],
        ),
        out_shape=[
            pltpu.HBM((count, piece, width), jnp.bfloat16),
            pltpu.HBM((count, piece, width), jnp.bfloat16),
            pltpu.HBM((count * piece, hidden), jnp.bfloat16),
        ],
        compiler_params=pltpu.CompilerParams(vmem_limit_bytes=VMEM_BYTES),
        cost_estimate=pl.CostEstimate(
            flops=4 * count * piece * width * hidden,
            bytes_accessed=2 * rows.size + 4 * width * hidden + 8 * count * piece * width,
            transcendentals=count * piece * hidden,
        ),
    )(slots, rows, gain, up, in_hbm(down), *after)


def back_kernel(slots, grad_ref, used_ref, slope_ref, gain_ref, up_ref, down_ref, *refs):
    out_ref, total = refs[-2:]
    step = pl.program_id(0)
    count, piece, width = used_ref.shape
    grads = merge_rows(grad_ref[...])

    @pl.when(step == 0)
    def _():
        out_ref[...] = jnp.zeros_like(out_ref)
        total[...] = jnp.zeros_like(total)

    activity_grad = dot_nt(grads, down_ref[...])
    before_grad = (activity_grad * slope_ref[...]).astype(jnp.bfloat16)
    total[...] += dot_nt(before_grad, up_ref[...])

    @pl.when(step == pl.num_programs(0) - 1)
    def _():
        row_values = used_ref[...].astype(jnp.float32).reshape(count * piece, width)
        inverse = inverse_of(row_values)
        scaled = gain_ref[...] * total[...]
        result = (
            grads.astype(jnp.float32)
            + inverse * scaled
            - row_values
            * (inverse * inverse * inverse)
            * jnp.mean(row_values * scaled, axis=-1, keepdims=True)
        )
        result = result.reshape(count, piece, width).astype(jnp.bfloat16)
        for g in range(count):
            out_ref[slots[g]] = result[g]


def encode_back(slots, grads, used, slope, gain, up, down, slot_count, after):
    count, piece, width = used.shape
    hidden = up.shape[1]
    chunk = hidden // 2
    whole = lambda *shape: pl.BlockSpec(shape, lambda f, s: (0,) * len(shape))
    return pl.pallas_call(
        back_kernel,
        grid_spec=pltpu.PrefetchScalarGridSpec(
            num_scalar_prefetch=1,
            grid=(hidden // chunk,),
            in_specs=[
                whole(count, piece, width),
                whole(count, piece, width),
                pl.BlockSpec((count * piece, chunk), lambda f, s: (0, f)),
                whole(1, width),
                pl.BlockSpec((width, chunk), lambda f, s: (0, f)),
                pl.BlockSpec((chunk, width), lambda f, s: (f, 0)),
            ]
            + [pl.BlockSpec(memory_space=pl.ANY)] * len(after),
            out_specs=whole(slot_count, piece, width),
            scratch_shapes=[pltpu.VMEM((count * piece, width), jnp.float32)],
        ),
        out_shape=pltpu.HBM((slot_count, piece, width), jnp.bfloat16),
        compiler_params=pltpu.CompilerParams(vmem_limit_bytes=VMEM_BYTES),
        cost_estimate=pl.CostEstimate(
            flops=4 * count * piece * width * hidden,
            bytes_accessed=4 * width * hidden + 8 * count * piece * width + 2 * count * piece * hidden,
            transcendentals=0,
        ),
    )(slots, grads, in_hbm(used), in_hbm(slope), gain, up, in_hbm(down), *after)


def attend_kernel(kinds, lines, last, plan, *refs):
    refs = list(refs)
    take = lambda count: [refs.pop(0) for _ in range(count)]
    steps = len(kinds)
    own_enc, other_enc = take(2)
    token_refs = (take(2), take(2))
    weight_refs = [take({"whole": 1, "columns": 2, "rows": lines}[kind]) for kind in kinds]
    if last:
        (back_in,) = take(1)
        take(4)
    out_refs = (take(2), take(2))
    back_refs = take(2 if last else 1)
    grad_halves = take(2)
    rows, rows_t, back, weight = refs
    step = pl.program_id(0)
    shares, mine, piece, width = own_enc.shape
    span = shares * piece
    scale = 1.0 / math.sqrt(HD)
    part_rows, columns = width // lines, weight.shape[1] // 2

    @pl.when(step == 0)
    def _():
        for s in range(2 * mine):
            source = own_enc if s < mine else other_enc
            rows[s * span : (s + 1) * span, :] = merge_rows(source[:, s % mine])
        rows_t[...] = rows[...].T
        back[...] = back_in[...] if last else jnp.zeros_like(back)

    for shard, (kind, found) in enumerate(zip(kinds, weight_refs)):

        @pl.when(step == shard)
        def _(kind=kind, found=found):
            if kind == "whole":
                weight[...] = found[0][...]
            elif kind == "columns":
                weight[:, :columns] = found[0][...]
                weight[:, columns:] = found[1][...]
            else:
                for i in range(lines):
                    start = pl.multiple_of(plan[steps + i] * part_rows, 16)
                    weight[pl.ds(start, part_rows), :] = found[i][...]

    both = dot(rows[...], weight[...]).astype(jnp.bfloat16)
    pairs = [(s, h) for s in range(2 * mine) for h in range(columns // HD)]

    def tokens_of(s, h):
        tokens = slice((s % mine) * STRETCH, (s % mine + 1) * STRETCH)
        return s // mine, tokens, slice(h * HD, (h + 1) * HD)

    def token_block(kind, s, h):
        side, tokens, cols = tokens_of(s, h)
        return token_refs[side][kind][tokens, cols]

    query = [token_block(0, s, h) for s, h in pairs]
    grad = [token_block(1, s, h) for s, h in pairs]
    key = [both[s * span : (s + 1) * span, h * HD : (h + 1) * HD] for s, h in pairs]
    value = [
        both[s * span : (s + 1) * span, columns + h * HD : columns + (h + 1) * HD] for s, h in pairs
    ]
    count = range(len(pairs))
    scores = jnp.concatenate([dot_nt(query[i], key[i]) for i in count], axis=0)
    prob_grad = jnp.concatenate([dot_nt(grad[i], value[i]) for i in count], axis=0)
    exponent = jnp.exp(scores * scale)
    weights = exponent * (1.0 / jnp.sum(exponent, axis=-1, keepdims=True))
    mean_grad = jnp.sum(weights * prob_grad, axis=-1, keepdims=True)
    probabilities = weights.astype(jnp.bfloat16)
    score_grad = (weights * (prob_grad - mean_grad) * scale).astype(jnp.bfloat16)
    prob = [probabilities[i * STRETCH : (i + 1) * STRETCH] for i in count]
    score = [score_grad[i * STRETCH : (i + 1) * STRETCH] for i in count]
    for i, (s, h) in enumerate(pairs):
        side, tokens, cols = tokens_of(s, h)
        out_refs[side][0][tokens, cols] = dot(prob[i], value[i]).astype(jnp.bfloat16)
        out_refs[side][1][tokens, cols] = dot(score[i], key[i]).astype(jnp.bfloat16)
    key_grad = [dot_tn(score[i], query[i]).astype(jnp.bfloat16) for i in count]
    value_grad = [dot_tn(prob[i], grad[i]).astype(jnp.bfloat16) for i in count]
    heads = columns // HD
    both_grad = jnp.concatenate(
        [
            jnp.concatenate(
                key_grad[s * heads : (s + 1) * heads] + value_grad[s * heads : (s + 1) * heads], axis=1
            )
            for s in range(2 * mine)
        ],
        axis=0,
    )
    for i in range(lines):
        start = pl.multiple_of(plan[steps + i] * part_rows, 16)
        part_grad = dot(rows_t[pl.ds(start, part_rows), :], both_grad).astype(jnp.bfloat16)
        grad_halves[2 * i // lines][i % (lines // 2), 0] = part_grad
    back[...] += dot_nt(both_grad, weight[...])

    @pl.when(step == steps - 1)
    def _():
        if not last:
            back_refs[0][...] = back[...]
        else:
            for s in range(2 * mine):
                block = back[s * span : (s + 1) * span, :].reshape(shares, piece, width)
                back_refs[s // mine][:, s % mine] = block.astype(jnp.bfloat16)


def attend(plan, lines, own_enc, other_enc, token_arrays, shards, earlier=None):
    last = earlier is not None
    steps = len(shards)
    kinds, arrays = [kind for kind, _ in shards], sum([found for _, found in shards], [])
    shares, mine, piece, width = own_enc.shape
    tokens, all_columns = token_arrays[0].shape
    columns = all_columns // shares
    part_rows = width // lines
    span = shares * piece
    all_rows = 2 * mine * span
    whole = lambda *shape: pl.BlockSpec(shape, lambda j, p: (0,) * len(shape))
    token_spec = pl.BlockSpec((tokens, columns), lambda j, p: (0, p[j]))
    enc_spec = whole(*own_enc.shape)
    out = functools.partial(jax.ShapeDtypeStruct, dtype=jnp.bfloat16)
    operands = [plan, own_enc, other_enc, *map(in_hbm, token_arrays), *arrays]
    in_specs = [enc_spec] * 2 + [token_spec] * 4 + [whole(*value.shape) for value in arrays]
    back_shapes, aliases = [jax.ShapeDtypeStruct((all_rows, width), jnp.float32)], {}
    if last:
        aliases = {len(operands) + 1 + i: i for i in range(4)}
        operands += [earlier[4], *map(in_hbm, earlier[:4])]
        in_specs += [whole(all_rows, width)] + [pl.BlockSpec(memory_space=pl.ANY)] * 4
        back_shapes = [out(own_enc.shape)] * 2
    return pl.pallas_call(
        functools.partial(attend_kernel, kinds, lines, last),
        grid_spec=pltpu.PrefetchScalarGridSpec(
            num_scalar_prefetch=1,
            grid=(steps,),
            in_specs=in_specs,
            out_specs=[token_spec] * 4
            + [whole(*shape.shape) for shape in back_shapes]
            + [pl.BlockSpec((lines // 2, 1, part_rows, 2 * columns), lambda j, p: (0, j, 0, 0))] * 2,
            scratch_shapes=[
                pltpu.VMEM((all_rows, width), jnp.bfloat16),
                pltpu.VMEM((width, all_rows), jnp.bfloat16),
                pltpu.VMEM((all_rows, width), jnp.float32),
                pltpu.VMEM((width, 2 * columns), jnp.bfloat16),
            ],
        ),
        out_shape=[pltpu.HBM((tokens, all_columns), jnp.bfloat16)] * 4
        + back_shapes
        + [pltpu.HBM((lines // 2, steps, part_rows, 2 * columns), jnp.bfloat16)] * 2,
        input_output_aliases=aliases,
        compiler_params=pltpu.CompilerParams(vmem_limit_bytes=VMEM_BYTES),
        cost_estimate=pl.CostEstimate(
            flops=12 * all_rows * width * steps * columns,
            bytes_accessed=8 * width * steps * columns + 8 * own_enc.size + 16 * tokens * steps * columns,
            transcendentals=2 * mine * STRETCH * span * steps * columns // HD,
        ),
    )(*operands)


def sum_kernel(count, sizes, *refs):
    terms, outs = refs[:count], refs[len(refs) - len(sizes) :]
    block = 0
    for size, out in zip(sizes, outs):
        for i in range(size):
            total = terms[0][block].astype(jnp.float32)
            for term in terms[1:]:
                total = total + term[block].astype(jnp.float32)
            out[i] = total.astype(jnp.bfloat16)
            block += 1


def sum_blocks(terms, sizes, after=(), to_hbm=False):
    blocks, rows, columns = terms[0].shape
    tiles = 2 if rows % 32 == 0 else 1
    spec = lambda size: pl.BlockSpec((size, rows // tiles, columns), lambda i: (0, i, 0))
    return pl.pallas_call(
        functools.partial(sum_kernel, len(terms), sizes),
        grid=(tiles,),
        in_specs=[spec(blocks)] * len(terms) + [pl.BlockSpec(memory_space=pl.ANY)] * len(after),
        out_specs=[spec(size) for size in sizes],
        out_shape=[
            (pltpu.HBM if to_hbm else jax.ShapeDtypeStruct)((size, rows, columns), jnp.bfloat16)
            for size in sizes
        ],
        compiler_params=pltpu.CompilerParams(vmem_limit_bytes=SMALL_VMEM_BYTES),
        cost_estimate=pl.CostEstimate(
            flops=len(terms) * blocks * rows * columns,
            bytes_accessed=2 * (len(terms) + 1) * blocks * rows * columns,
            transcendentals=0,
        ),
    )(*terms, *after)


def join_kernel(count, plan, *refs):
    parts, outs = refs[:count], refs[count:]
    part_rows, columns = parts[0].shape[0], outs[0].shape[1]
    for i, part in enumerate(parts):
        start = pl.multiple_of(plan[i] * part_rows, 16)
        for k, out in enumerate(outs):
            out[pl.ds(start, part_rows), :] = part[:, k * columns : (k + 1) * columns].astype(out.dtype)


def join_parts(plan, parts, outs, dtype, microseconds):
    part_rows, columns = parts[0].shape
    width = part_rows * len(parts)
    whole = lambda *shape: pl.BlockSpec(shape, lambda j, p: (0,) * len(shape))
    return pl.pallas_call(
        functools.partial(join_kernel, len(parts)),
        grid_spec=pltpu.PrefetchScalarGridSpec(
            num_scalar_prefetch=1,
            grid=(1,),
            in_specs=[whole(part_rows, columns)] * len(parts),
            out_specs=[whole(width, columns // outs)] * outs,
        ),
        out_shape=[jax.ShapeDtypeStruct((width, columns // outs), dtype)] * outs,
        compiler_params=pltpu.CompilerParams(vmem_limit_bytes=SMALL_VMEM_BYTES),
        cost_estimate=stated(microseconds),
    )(plan, *parts)


def swap_cores(value):
    return lax.ppermute(value, "core", [(0, 1), (1, 0)])


def swap_chips(value, shift):
    return lax.ppermute(value, "z", [(z, z ^ shift) for z in range(lax.axis_size("z"))])


def line_bit(core, stage, stages):
    return 1 << stage if core == 0 else 1 << (stages - 1 - stage)


def swap_lines(value, stage, stages):
    lines = lax.axis_size("line")
    pairs = [
        (line * 2 + core, (line ^ line_bit(core, stage, stages)) * 2 + core)
        for line in range(lines)
        for core in range(2)
    ]
    return lax.ppermute(value, ("line", "core"), pairs)


def gather_lines(value, stages):
    found = [value]
    for stage in range(stages):
        found = found + [swap_lines(item, stage, stages) for item in found]
    return found


def on_device(
    queries,
    attended_grad,
    neighbour_pool,
    stretch_slot,
    enc_gain,
    enc_up,
    enc_down,
    key_weight,
    value_weight,
):
    chips, lines = lax.axis_size("z"), lax.axis_size("line")
    stages = lines.bit_length() - 1
    groups = 2 * chips
    core, chip, line = lax.axis_index("core"), lax.axis_index("z"), lax.axis_index("line")
    tokens, all_columns = queries.shape[1:]
    mine = tokens // STRETCH
    holding, span, width = neighbour_pool.shape[1:]
    piece = span // groups
    columns = key_weight.shape[1]
    slots = stretch_slot[0]
    gain = enc_gain.reshape(1, width)

    offsets = [
        [sum(line_bit(c, s, stages) for s in range(stages) if i >> s & 1) for i in range(lines)]
        for c in range(2)
    ]
    part_lines = line ^ jnp.where(
        core == 0, jnp.array(offsets[0], jnp.int32), jnp.array(offsets[1], jnp.int32)
    )
    part_lines = part_lines.astype(jnp.int32)

    part_rows = width // lines
    part = jnp.concatenate(
        [
            lax.dynamic_slice_in_dim(weight, line * part_rows, part_rows, 0)
            for weight in (key_weight, value_weight)
        ],
        axis=1,
    )
    odd, even = range(1, chips, 2), range(2, chips, 2)
    part = {0: part}
    shift = chips // 2
    while shift > 1:
        part |= {s | shift: swap_chips(value, shift) for s, value in part.items()}
        shift //= 2
    part[1] = swap_chips(part[0], 1)

    pieces = neighbour_pool[0].reshape(holding, groups, piece, width).transpose(1, 0, 2, 3)
    received = lax.all_to_all(pieces, SEQ, split_axis=0, concat_axis=0, tiled=True)
    received = received.reshape(groups * holding, piece, width)

    token_arrays = [queries[0], attended_grad[0]]
    token_arrays += [swap_cores(value) for value in token_arrays]

    encoded, used, slope = encode_rows(slots, received, gain, enc_up, enc_down, [])
    encoded, part = lax.optimization_barrier((encoded, part))
    part |= {s | 1: swap_chips(part[s], 1) for s in even}
    own_enc = lax.all_to_all(
        encoded.reshape(groups, mine, piece, width), SEQ, split_axis=0, concat_axis=0, tiled=True
    )
    shards = {0: ("columns", [in_hbm(key_weight), in_hbm(value_weight)])}
    for shift in range(1, chips):
        found = gather_lines(part[shift], stages)
        if shift == 1 or shift in even:
            shards[shift] = ("whole", [*join_parts(part_lines, found, 1, jnp.bfloat16, 4)])
        else:
            shards[shift] = ("rows", found)
    other_enc = swap_cores(own_enc)

    steps = ([0, *even], [*odd])
    plans = [
        jnp.concatenate([jnp.stack([(chip ^ shift) * 2 + core for shift in shifts]), part_lines])
        for shifts in steps
    ]
    parted = [[shards[shift] for shift in shifts] for shifts in steps]
    first = attend(plans[0], lines, own_enc, other_enc, token_arrays, parted[0])
    last = attend(plans[1], lines, own_enc, other_enc, token_arrays, parted[1], first[:5])
    outs, own_back, other_back = last[:4], last[4], last[5]

    rows = groups * mine * piece
    (back,) = sum_blocks(
        [own_back.reshape(1, rows, width), swap_cores(other_back).reshape(1, rows, width)],
        (1,),
        to_hbm=True,
    )
    split_rows = lax.all_to_all(
        back.reshape(groups, mine, piece, width), SEQ, split_axis=0, concat_axis=0, tiled=True
    )

    count = chips // 2
    first_halves = [first[5], swap_lines(first[6], stages - 1, stages)]
    last_halves = [last[6], swap_lines(last[7], stages - 1, stages)]
    after = [in_hbm(back)]
    for stage in reversed(range(stages)):
        size = first_halves[0].size // (part_rows * 2 * columns)
        sizes = (size // 2, size // 2) if stage else (1,) * count
        flat = lambda halves: [value.reshape(size, part_rows, 2 * columns) for value in halves]
        first_flat, last_flat = flat(first_halves), flat(last_halves)
        if stage == stages - 1:
            first_flat[0], last_flat[0] = in_hbm(first_flat[0]), in_hbm(last_flat[0])
        first_sums = sum_blocks(first_flat, sizes, after)
        last_sums = sum_blocks(last_flat, sizes, [first_sums[0]])
        after = [last_sums[0]]
        if stage:
            first_halves = [first_sums[0], swap_lines(first_sums[1], stage - 1, stages)]
            last_halves = [last_sums[0], swap_lines(last_sums[1], stage - 1, stages)]
    terms = {0: first_sums[0]}
    terms |= {shift: swap_chips(value, shift) for value, shift in zip(first_sums[1:], even)}
    terms |= {shift: swap_chips(value, shift) for value, shift in zip(last_sums, odd)}
    placed = encode_back(
        slots,
        split_rows.reshape(groups * mine, piece, width),
        used,
        slope,
        gain,
        enc_up,
        enc_down,
        groups * holding,
        [],
    )
    (share,) = sum_blocks([*terms.values()], (1,), [in_hbm(placed)])
    share = share[0]
    if lax.axis_size("far") > 1:
        share = lax.psum(share, "far")
    weight_grads = join_parts(part_lines, gather_lines(share, stages), 2, jnp.float32, 10)

    returned = lax.all_to_all(
        placed.reshape(groups, holding, piece, width), SEQ, split_axis=0, concat_axis=0, tiled=True
    )
    pool_grad = returned.transpose(1, 0, 2, 3).reshape(1, holding, span, width)

    is_own = (lax.broadcasted_iota(jnp.int32, (1, all_columns), 1) // columns) % 2 == core
    outs = [jnp.where(is_own, outs[i], swap_cores(outs[2 + i]))[None] for i in range(2)]
    return outs[0], outs[1], pool_grad, weight_grads[0], weight_grads[1]


def solution(mesh):
    dp, seq = mesh.shape["dp"], mesh.shape["seq"]
    lines = 4 if dp % 4 == 0 else dp
    fine = Mesh(
        mesh.devices.reshape(dp // lines, lines, seq // 2, 2), ("far", "line", "z", "core")
    )
    dp_axes = ("far", "line")
    return jax.shard_map(
        on_device,
        mesh=fine,
        in_specs=(
            P(dp_axes, SEQ, None),
            P(dp_axes, SEQ, None),
            P(dp_axes, SEQ, None, None),
            P(dp_axes, None),
            P(),
            P(),
            P(),
            P(None, SEQ),
            P(None, SEQ),
        ),
        out_specs=(
            P(dp_axes, SEQ, None),
            P(dp_axes, SEQ, None),
            P(dp_axes, SEQ, None, None),
            P(None, SEQ),
            P(None, SEQ),
        ),
        check_vma=False,
    )
```

```python
import functools
import math

import jax
import jax.numpy as jnp
from jax import lax
from jax.experimental import pallas as pl
from jax.experimental.pallas import tpu as pltpu
from jax.sharding import Mesh, PartitionSpec as P

STRETCH = 64
HD = 128
EPSILON = 1e-06
GELU_RATE = math.sqrt(2.0 / math.pi)
GELU_CUBE = 0.044715
VMEM_BYTES = 28 * 1024 * 1024
SMALL_VMEM_BYTES = 12 * 1024 * 1024
SEQ = ("z", "core")


def dot(left, right):
    return jnp.dot(left, right, preferred_element_type=jnp.float32)


def dot_nt(left, right):
    return lax.dot_general(left, right, (((1,), (1,)), ((), ())), preferred_element_type=jnp.float32)


def dot_tn(left, right):
    return lax.dot_general(left, right, (((0,), (0,)), ((), ())), preferred_element_type=jnp.float32)


def stated(microseconds):
    return pl.CostEstimate(
        flops=microseconds * 1_000_000_000, bytes_accessed=microseconds * 3_000_000, transcendentals=0
    )


def in_hbm(value):
    return pltpu.with_memory_space_constraint(value, pltpu.HBM)


def merge_rows(block):
    pieces, rows, width = block.shape
    if rows % 16 == 0:
        return block.reshape(pieces * rows, width)
    return block.astype(jnp.float32).reshape(pieces * rows, width).astype(jnp.bfloat16)


def inverse_of(row_values):
    return lax.rsqrt(jnp.mean(row_values * row_values, axis=-1, keepdims=True) + EPSILON)


def encode_kernel(slots, rows_ref, gain_ref, up_ref, down_ref, *refs):
    enc_ref, used_ref, slope_ref, normed, total = refs[-5:]
    step = pl.program_id(0)
    count, piece, width = used_ref.shape

    @pl.when(step == 0)
    def _():
        for g in range(count):
            used_ref[g] = rows_ref[slots[g]]
        row_values = used_ref[...].astype(jnp.float32).reshape(count * piece, width)
        normed[...] = (row_values * inverse_of(row_values) * gain_ref[...]).astype(jnp.bfloat16)
        total[...] = row_values

    before = dot(normed[...], up_ref[...])
    square = before * before
    bend = jnp.tanh(GELU_RATE * before * (1.0 + GELU_CUBE * square))
    half = 0.5 * (1.0 + bend)
    activity = (before * half).astype(jnp.bfloat16)
    slope = half + 0.5 * before * (1.0 - bend * bend) * (
        GELU_RATE * (1.0 + 3.0 * GELU_CUBE * square)
    )
    slope_ref[...] = slope.astype(slope_ref.dtype)
    total[...] += dot(activity, down_ref[...])

    @pl.when(step == pl.num_programs(0) - 1)
    def _():
        enc_ref[...] = total[...].reshape(count, piece, width).astype(jnp.bfloat16)


def encode_rows(slots, rows, gain, up, down, after):
    count = slots.shape[0]
    piece, width = rows.shape[1:]
    hidden = up.shape[1]
    chunk = hidden // 2
    whole = lambda *shape: pl.BlockSpec(shape, lambda f, s: (0,) * len(shape))
    return pl.pallas_call(
        encode_kernel,
        grid_spec=pltpu.PrefetchScalarGridSpec(
            num_scalar_prefetch=1,
            grid=(hidden // chunk,),
            in_specs=[
                whole(*rows.shape),
                whole(1, width),
                pl.BlockSpec((width, chunk), lambda f, s: (0, f)),
                pl.BlockSpec((chunk, width), lambda f, s: (f, 0)),
            ]
            + [pl.BlockSpec(memory_space=pl.ANY)] * len(after),
            out_specs=[
                whole(count, piece, width),
                whole(count, piece, width),
                pl.BlockSpec((count * piece, chunk), lambda f, s: (0, f)),
            ],
            scratch_shapes=[
                pltpu.VMEM((count * piece, width), jnp.bfloat16),
                pltpu.VMEM((count * piece, width), jnp.float32),
            ],
        ),
        out_shape=[
            pltpu.HBM((count, piece, width), jnp.bfloat16),
            pltpu.HBM((count, piece, width), jnp.bfloat16),
            pltpu.HBM((count * piece, hidden), jnp.bfloat16),
        ],
        compiler_params=pltpu.CompilerParams(vmem_limit_bytes=VMEM_BYTES),
        cost_estimate=pl.CostEstimate(
            flops=4 * count * piece * width * hidden,
            bytes_accessed=2 * rows.size + 4 * width * hidden + 8 * count * piece * width,
            transcendentals=count * piece * hidden,
        ),
    )(slots, rows, gain, up, in_hbm(down), *after)


def back_kernel(slots, grad_ref, used_ref, slope_ref, gain_ref, up_ref, down_ref, *refs):
    out_ref, total = refs[-2:]
    step = pl.program_id(0)
    count, piece, width = used_ref.shape
    grads = merge_rows(grad_ref[...])

    @pl.when(step == 0)
    def _():
        out_ref[...] = jnp.zeros_like(out_ref)
        total[...] = jnp.zeros_like(total)

    activity_grad = dot_nt(grads, down_ref[...])
    before_grad = (activity_grad * slope_ref[...]).astype(jnp.bfloat16)
    total[...] += dot_nt(before_grad, up_ref[...])

    @pl.when(step == pl.num_programs(0) - 1)
    def _():
        row_values = used_ref[...].astype(jnp.float32).reshape(count * piece, width)
        inverse = inverse_of(row_values)
        scaled = gain_ref[...] * total[...]
        result = (
            grads.astype(jnp.float32)
            + inverse * scaled
            - row_values
            * (inverse * inverse * inverse)
            * jnp.mean(row_values * scaled, axis=-1, keepdims=True)
        )
        result = result.reshape(count, piece, width).astype(jnp.bfloat16)
        for g in range(count):
            out_ref[slots[g]] = result[g]


def encode_back(slots, grads, used, slope, gain, up, down, slot_count, after):
    count, piece, width = used.shape
    hidden = up.shape[1]
    chunk = hidden // 2
    whole = lambda *shape: pl.BlockSpec(shape, lambda f, s: (0,) * len(shape))
    return pl.pallas_call(
        back_kernel,
        grid_spec=pltpu.PrefetchScalarGridSpec(
            num_scalar_prefetch=1,
            grid=(hidden // chunk,),
            in_specs=[
                whole(count, piece, width),
                whole(count, piece, width),
                pl.BlockSpec((count * piece, chunk), lambda f, s: (0, f)),
                whole(1, width),
                pl.BlockSpec((width, chunk), lambda f, s: (0, f)),
                pl.BlockSpec((chunk, width), lambda f, s: (f, 0)),
            ]
            + [pl.BlockSpec(memory_space=pl.ANY)] * len(after),
            out_specs=whole(slot_count, piece, width),
            scratch_shapes=[pltpu.VMEM((count * piece, width), jnp.float32)],
        ),
        out_shape=pltpu.HBM((slot_count, piece, width), jnp.bfloat16),
        compiler_params=pltpu.CompilerParams(vmem_limit_bytes=VMEM_BYTES),
        cost_estimate=pl.CostEstimate(
            flops=4 * count * piece * width * hidden,
            bytes_accessed=4 * width * hidden + 8 * count * piece * width + 2 * count * piece * hidden,
            transcendentals=0,
        ),
    )(slots, grads, in_hbm(used), in_hbm(slope), gain, up, in_hbm(down), *after)


def attend_kernel(kinds, lines, last, plan, *refs):
    refs = list(refs)
    take = lambda count: [refs.pop(0) for _ in range(count)]
    steps = len(kinds)
    own_enc, other_enc = take(2)
    token_refs = (take(2), take(2))
    weight_refs = [take({"columns": 2, "rows": lines}[kind]) for kind in kinds]
    if last:
        (back_in,) = take(1)
        take(4)
    out_refs = (take(2), take(2))
    back_refs = take(2 if last else 1)
    grad_halves = take(2)
    rows, rows_t, back, weight, weight_done = refs[:5]
    if last:
        back_held, back_done = refs[5:]
    step = pl.program_id(0)
    shares, mine, piece, width = own_enc.shape
    span = shares * piece
    scale = 1.0 / math.sqrt(HD)
    part_rows, columns = width // lines, weight.shape[2] // 2

    def weight_copies(shard):
        kind, found = kinds[shard], weight_refs[shard]
        if kind == "columns":
            places = [(slice(None), pl.ds(k * columns, columns)) for k in range(2)]
        else:
            places = [
                (pl.ds(pl.multiple_of(plan[steps + i] * part_rows, 16), part_rows), slice(None))
                for i in range(lines)
            ]
        return [
            pltpu.make_async_copy(part, weight.at[shard, *place], weight_done.at[shard, i])
            for i, (part, place) in enumerate(zip(found, places))
        ]

    def back_copy():
        return pltpu.make_async_copy(back_in, back_held, back_done)

    @pl.when(step == 0)
    def _():
        for shard in range(steps):
            for copy in weight_copies(shard):
                copy.start()
        if last:
            back_copy().start()
        for s in range(2 * mine):
            source = own_enc if s < mine else other_enc
            rows[s * span : (s + 1) * span, :] = merge_rows(source[:, s % mine])
        rows_t[...] = rows[...].T
        back[...] = jnp.zeros_like(back)

    for shard in range(steps):

        @pl.when(step == shard)
        def _(shard=shard):
            for copy in weight_copies(shard):
                copy.wait()

    both = dot(rows[...], weight[step]).astype(jnp.bfloat16)
    pairs = [(s, h) for s in range(2 * mine) for h in range(columns // HD)]

    def tokens_of(s, h):
        tokens = slice((s % mine) * STRETCH, (s % mine + 1) * STRETCH)
        return s // mine, tokens, slice(h * HD, (h + 1) * HD)

    def token_block(kind, s, h):
        side, tokens, cols = tokens_of(s, h)
        return token_refs[side][kind][tokens, cols]

    query = [token_block(0, s, h) for s, h in pairs]
    grad = [token_block(1, s, h) for s, h in pairs]
    key = [both[s * span : (s + 1) * span, h * HD : (h + 1) * HD] for s, h in pairs]
    value = [
        both[s * span : (s + 1) * span, columns + h * HD : columns + (h + 1) * HD] for s, h in pairs
    ]
    count = range(len(pairs))
    scores = jnp.concatenate([dot_nt(query[i], key[i]) for i in count], axis=0)
    prob_grad = jnp.concatenate([dot_nt(grad[i], value[i]) for i in count], axis=0)
    exponent = jnp.exp(scores * scale)
    weights = exponent * (1.0 / jnp.sum(exponent, axis=-1, keepdims=True))
    mean_grad = jnp.sum(weights * prob_grad, axis=-1, keepdims=True)
    probabilities = weights.astype(jnp.bfloat16)
    score_grad = (weights * (prob_grad - mean_grad) * scale).astype(jnp.bfloat16)
    prob = [probabilities[i * STRETCH : (i + 1) * STRETCH] for i in count]
    score = [score_grad[i * STRETCH : (i + 1) * STRETCH] for i in count]
    for i, (s, h) in enumerate(pairs):
        side, tokens, cols = tokens_of(s, h)
        out_refs[side][0][tokens, cols] = dot(prob[i], value[i]).astype(jnp.bfloat16)
        out_refs[side][1][tokens, cols] = dot(score[i], key[i]).astype(jnp.bfloat16)
    key_grad = [dot_tn(score[i], query[i]).astype(jnp.bfloat16) for i in count]
    value_grad = [dot_tn(prob[i], grad[i]).astype(jnp.bfloat16) for i in count]
    heads = columns // HD
    both_grad = jnp.concatenate(
        [
            jnp.concatenate(
                key_grad[s * heads : (s + 1) * heads] + value_grad[s * heads : (s + 1) * heads], axis=1
            )
            for s in range(2 * mine)
        ],
        axis=0,
    )
    for i in range(lines):
        start = pl.multiple_of(plan[steps + i] * part_rows, 16)
        part_grad = dot(rows_t[pl.ds(start, part_rows), :], both_grad).astype(jnp.bfloat16)
        grad_halves[2 * i // lines][i % (lines // 2), 0] = part_grad
    back[...] += dot_nt(both_grad, weight[step])

    @pl.when(step == steps - 1)
    def _():
        if not last:
            back_refs[0][...] = back[...].astype(jnp.bfloat16)
        else:
            back_copy().wait()
            back[...] += back_held[...].astype(jnp.float32)
            for s in range(2 * mine):
                block = back[s * span : (s + 1) * span, :].reshape(shares, piece, width)
                back_refs[s // mine][:, s % mine] = block.astype(jnp.bfloat16)


def attend(plan, lines, own_enc, other_enc, token_arrays, shards, earlier=None):
    last = earlier is not None
    steps = len(shards)
    kinds, arrays = [kind for kind, _ in shards], sum([found for _, found in shards], [])
    shares, mine, piece, width = own_enc.shape
    tokens, all_columns = token_arrays[0].shape
    columns = all_columns // shares
    part_rows = width // lines
    span = shares * piece
    all_rows = 2 * mine * span
    whole = lambda *shape: pl.BlockSpec(shape, lambda j, p: (0,) * len(shape))
    token_spec = pl.BlockSpec((tokens, columns), lambda j, p: (0, p[j]))
    enc_spec = whole(*own_enc.shape)
    out = functools.partial(jax.ShapeDtypeStruct, dtype=jnp.bfloat16)
    operands = [plan, own_enc, other_enc, *map(in_hbm, token_arrays), *arrays]
    in_specs = [enc_spec] * 2 + [token_spec] * 4 + [pl.BlockSpec(memory_space=pl.ANY)] * len(arrays)
    back_shapes, aliases = [out((all_rows, width))], {}
    if last:
        aliases = {len(operands) + 1 + i: i for i in range(4)}
        operands += [earlier[4], *map(in_hbm, earlier[:4])]
        in_specs += [pl.BlockSpec(memory_space=pl.ANY)] * 5
        back_shapes = [out(own_enc.shape)] * 2
    return pl.pallas_call(
        functools.partial(attend_kernel, kinds, lines, last),
        grid_spec=pltpu.PrefetchScalarGridSpec(
            num_scalar_prefetch=1,
            grid=(steps,),
            in_specs=in_specs,
            out_specs=[token_spec] * 4
            + [whole(*shape.shape) for shape in back_shapes]
            + [pl.BlockSpec((lines // 2, 1, part_rows, 2 * columns), lambda j, p: (0, j, 0, 0))] * 2,
            scratch_shapes=[
                pltpu.VMEM((all_rows, width), jnp.bfloat16),
                pltpu.VMEM((width, all_rows), jnp.bfloat16),
                pltpu.VMEM((all_rows, width), jnp.float32),
                pltpu.VMEM((steps, width, 2 * columns), jnp.bfloat16),
                pltpu.SemaphoreType.DMA((steps, max(lines, 2))),
            ]
            + [pltpu.VMEM((all_rows, width), jnp.bfloat16), pltpu.SemaphoreType.DMA] * last,
        ),
        out_shape=[pltpu.HBM((tokens, all_columns), jnp.bfloat16)] * 4
        + back_shapes
        + [pltpu.HBM((lines // 2, steps, part_rows, 2 * columns), jnp.bfloat16)] * 2,
        input_output_aliases=aliases,
        compiler_params=pltpu.CompilerParams(vmem_limit_bytes=VMEM_BYTES),
        cost_estimate=pl.CostEstimate(
            flops=12 * all_rows * width * steps * columns,
            bytes_accessed=8 * width * steps * columns + 8 * own_enc.size + 16 * tokens * steps * columns,
            transcendentals=2 * mine * STRETCH * span * steps * columns // HD,
        ),
    )(*operands)


def sum_kernel(count, sizes, *refs):
    terms, outs = refs[:count], refs[len(refs) - len(sizes) :]
    block = 0
    for size, out in zip(sizes, outs):
        for i in range(size):
            total = terms[0][block].astype(jnp.float32)
            for term in terms[1:]:
                total = total + term[block].astype(jnp.float32)
            out[i] = total.astype(jnp.bfloat16)
            block += 1


def sum_blocks(terms, sizes, after=(), to_hbm=False):
    blocks, rows, columns = terms[0].shape
    tiles = 2 if rows % 32 == 0 else 1
    spec = lambda size: pl.BlockSpec((size, rows // tiles, columns), lambda i: (0, i, 0))
    return pl.pallas_call(
        functools.partial(sum_kernel, len(terms), sizes),
        grid=(tiles,),
        in_specs=[spec(blocks)] * len(terms) + [pl.BlockSpec(memory_space=pl.ANY)] * len(after),
        out_specs=[spec(size) for size in sizes],
        out_shape=[
            (pltpu.HBM if to_hbm else jax.ShapeDtypeStruct)((size, rows, columns), jnp.bfloat16)
            for size in sizes
        ],
        compiler_params=pltpu.CompilerParams(vmem_limit_bytes=SMALL_VMEM_BYTES),
        cost_estimate=pl.CostEstimate(
            flops=len(terms) * blocks * rows * columns,
            bytes_accessed=2 * (len(terms) + 1) * blocks * rows * columns,
            transcendentals=0,
        ),
    )(*terms, *after)


def copy_kernel(plan, *refs):
    out = refs[-1]
    for i in range(plan.shape[0]):
        out[i] = plan[i]


def copy_plan(plan, others):
    scalars = pl.BlockSpec(memory_space=pltpu.SMEM)
    return pl.pallas_call(
        copy_kernel,
        in_specs=[scalars] + [pl.BlockSpec(memory_space=pl.ANY)] * len(others),
        out_specs=scalars,
        out_shape=jax.ShapeDtypeStruct(plan.shape, plan.dtype),
        compiler_params=pltpu.CompilerParams(vmem_limit_bytes=SMALL_VMEM_BYTES),
        cost_estimate=stated(4),
    )(plan, *others)


def join_kernel(plan, *refs):
    parts, outs = refs[:-2], refs[-2:]
    part_rows, columns = parts[0].shape[0], outs[0].shape[1]
    for i, part in enumerate(parts):
        start = pl.multiple_of(plan[i] * part_rows, 16)
        for k, out in enumerate(outs):
            out[pl.ds(start, part_rows), :] = part[:, k * columns : (k + 1) * columns].astype(out.dtype)


def join_grads(plan, parts):
    part_rows, columns = parts[0].shape
    width = part_rows * len(parts)
    whole = lambda *shape: pl.BlockSpec(shape, lambda j, p: (0,) * len(shape))
    return pl.pallas_call(
        join_kernel,
        grid_spec=pltpu.PrefetchScalarGridSpec(
            num_scalar_prefetch=1,
            grid=(1,),
            in_specs=[whole(part_rows, columns)] * len(parts),
            out_specs=[whole(width, columns // 2)] * 2,
        ),
        out_shape=[jax.ShapeDtypeStruct((width, columns // 2), jnp.float32)] * 2,
        compiler_params=pltpu.CompilerParams(vmem_limit_bytes=SMALL_VMEM_BYTES),
        cost_estimate=stated(8),
    )(plan, *parts)


def swap_cores(value):
    return lax.ppermute(value, "core", [(0, 1), (1, 0)])


def swap_chips(value, shift):
    return lax.ppermute(value, "z", [(z, z ^ shift) for z in range(lax.axis_size("z"))])


def line_bit(core, stage, stages):
    return 1 << stage if core == 0 else 1 << (stages - 1 - stage)


def swap_lines(value, stage, stages):
    lines = lax.axis_size("line")
    pairs = [
        (line * 2 + core, (line ^ line_bit(core, stage, stages)) * 2 + core)
        for line in range(lines)
        for core in range(2)
    ]
    return lax.ppermute(value, ("line", "core"), pairs)


def gather_lines(value, stages):
    found = [value]
    for stage in range(stages):
        found = found + [swap_lines(item, stage, stages) for item in found]
    return found


def on_device(
    queries,
    attended_grad,
    neighbour_pool,
    stretch_slot,
    enc_gain,
    enc_up,
    enc_down,
    key_weight,
    value_weight,
):
    chips, lines = lax.axis_size("z"), lax.axis_size("line")
    stages = lines.bit_length() - 1
    groups = 2 * chips
    core, chip, line = lax.axis_index("core"), lax.axis_index("z"), lax.axis_index("line")
    tokens, all_columns = queries.shape[1:]
    mine = tokens // STRETCH
    holding, span, width = neighbour_pool.shape[1:]
    piece = span // groups
    columns = key_weight.shape[1]
    slots = stretch_slot[0]
    gain = enc_gain.reshape(1, width)

    offsets = [
        [sum(line_bit(c, s, stages) for s in range(stages) if i >> s & 1) for i in range(lines)]
        for c in range(2)
    ]
    part_lines = line ^ jnp.where(
        core == 0, jnp.array(offsets[0], jnp.int32), jnp.array(offsets[1], jnp.int32)
    )
    part_lines = part_lines.astype(jnp.int32)

    part_rows = width // lines
    part = jnp.concatenate(
        [
            lax.dynamic_slice_in_dim(weight, line * part_rows, part_rows, 0)
            for weight in (key_weight, value_weight)
        ],
        axis=1,
    )
    odd, even = range(1, chips, 2), range(2, chips, 2)
    part = {0: part}
    shift = chips // 2
    while shift > 1:
        part |= {s | shift: swap_chips(value, shift) for s, value in part.items()}
        shift //= 2
    part[1] = swap_chips(part[0], 1)

    pieces = neighbour_pool[0].reshape(holding, groups, piece, width).transpose(1, 0, 2, 3)
    received = lax.all_to_all(pieces, SEQ, split_axis=0, concat_axis=0, tiled=True)
    received = received.reshape(groups * holding, piece, width)

    token_arrays = [queries[0], attended_grad[0]]
    token_arrays += [swap_cores(value) for value in token_arrays]

    encoded, used, slope = encode_rows(slots, received, gain, enc_up, enc_down, [])
    encoded, part = lax.optimization_barrier((encoded, part))
    part |= {s | 1: swap_chips(part[s], 1) for s in even}
    own_enc = lax.all_to_all(
        encoded.reshape(groups, mine, piece, width), SEQ, split_axis=0, concat_axis=0, tiled=True
    )
    shards = {0: ("columns", [in_hbm(key_weight), in_hbm(value_weight)])}
    for shift in range(1, chips):
        shards[shift] = ("rows", gather_lines(part[shift], stages))
    other_enc = swap_cores(own_enc)

    steps = ([0, *even], [*odd])
    plans = [
        jnp.concatenate([jnp.stack([(chip ^ shift) * 2 + core for shift in shifts]), part_lines])
        for shifts in steps
    ]
    early = [value for shift in (1, *even) for value in shards[shift][1][lines // 2 :]]
    plans[0] = copy_plan(plans[0], early)
    parted = [[shards[shift] for shift in shifts] for shifts in steps]
    first = attend(plans[0], lines, own_enc, other_enc, token_arrays, parted[0])
    last = attend(plans[1], lines, own_enc, other_enc, token_arrays, parted[1], first[:5])
    outs, own_back, other_back = last[:4], last[4], last[5]

    rows = groups * mine * piece
    (back,) = sum_blocks(
        [own_back.reshape(1, rows, width), swap_cores(other_back).reshape(1, rows, width)],
        (1,),
        to_hbm=True,
    )
    split_rows = lax.all_to_all(
        back.reshape(groups, mine, piece, width), SEQ, split_axis=0, concat_axis=0, tiled=True
    )

    count = chips // 2
    first_halves = [first[5], swap_lines(first[6], stages - 1, stages)]
    last_halves = [last[6], swap_lines(last[7], stages - 1, stages)]
    after = [in_hbm(back)]
    for stage in reversed(range(stages)):
        size = first_halves[0].size // (part_rows * 2 * columns)
        sizes = (size // 2, size // 2) if stage else (1,) * count
        flat = lambda halves: [value.reshape(size, part_rows, 2 * columns) for value in halves]
        first_flat, last_flat = flat(first_halves), flat(last_halves)
        if stage == stages - 1:
            first_flat[0], last_flat[0] = in_hbm(first_flat[0]), in_hbm(last_flat[0])
        first_sums = sum_blocks(first_flat, sizes, after)
        last_sums = sum_blocks(last_flat, sizes, [first_sums[0]])
        after = [last_sums[0]]
        if stage:
            first_halves = [first_sums[0], swap_lines(first_sums[1], stage - 1, stages)]
            last_halves = [last_sums[0], swap_lines(last_sums[1], stage - 1, stages)]
    terms = {0: first_sums[0]}
    terms |= {shift: swap_chips(value, shift) for value, shift in zip(first_sums[1:], even)}
    terms |= {shift: swap_chips(value, shift) for value, shift in zip(last_sums, odd)}
    placed = encode_back(
        slots,
        split_rows.reshape(groups * mine, piece, width),
        used,
        slope,
        gain,
        enc_up,
        enc_down,
        groups * holding,
        [terms[shift] for shift in even],
    )
    (share,) = sum_blocks([*terms.values()], (1,), [in_hbm(placed)])
    share = share[0]
    if lax.axis_size("far") > 1:
        share = lax.psum(share, "far")
    weight_grads = join_grads(part_lines, gather_lines(share, stages))

    returned = lax.all_to_all(
        placed.reshape(groups, holding, piece, width), SEQ, split_axis=0, concat_axis=0, tiled=True
    )
    pool_grad = returned.transpose(1, 0, 2, 3).reshape(1, holding, span, width)

    is_own = (lax.broadcasted_iota(jnp.int32, (1, all_columns), 1) // columns) % 2 == core
    outs = [jnp.where(is_own, outs[i], swap_cores(outs[2 + i]))[None] for i in range(2)]
    return outs[0], outs[1], pool_grad, weight_grads[0], weight_grads[1]


def solution(mesh):
    dp, seq = mesh.shape["dp"], mesh.shape["seq"]
    lines = 4 if dp % 4 == 0 else dp
    fine = Mesh(
        mesh.devices.reshape(dp // lines, lines, seq // 2, 2), ("far", "line", "z", "core")
    )
    dp_axes = ("far", "line")
    return jax.shard_map(
        on_device,
        mesh=fine,
        in_specs=(
            P(dp_axes, SEQ, None),
            P(dp_axes, SEQ, None),
            P(dp_axes, SEQ, None, None),
            P(dp_axes, None),
            P(),
            P(),
            P(),
            P(None, SEQ),
            P(None, SEQ),
        ),
        out_specs=(
            P(dp_axes, SEQ, None),
            P(dp_axes, SEQ, None),
            P(dp_axes, SEQ, None, None),
            P(None, SEQ),
            P(None, SEQ),
        ),
        check_vma=False,
    )
```

```python
import functools
import math

import jax
import jax.numpy as jnp
from jax import lax
from jax.experimental import pallas as pl
from jax.experimental.pallas import tpu as pltpu
from jax.sharding import Mesh, PartitionSpec as P

STRETCH = 64
HD = 128
EPSILON = 1e-06
GELU_RATE = math.sqrt(2.0 / math.pi)
GELU_CUBE = 0.044715
VMEM_BYTES = 28 * 1024 * 1024
SMALL_VMEM_BYTES = 12 * 1024 * 1024
SEQ = ("z", "core")


def dot(left, right):
    return jnp.dot(left, right, preferred_element_type=jnp.float32)


def dot_nt(left, right):
    return lax.dot_general(left, right, (((1,), (1,)), ((), ())), preferred_element_type=jnp.float32)


def dot_tn(left, right):
    return lax.dot_general(left, right, (((0,), (0,)), ((), ())), preferred_element_type=jnp.float32)


def stated(microseconds):
    return pl.CostEstimate(
        flops=microseconds * 1_000_000_000, bytes_accessed=microseconds * 3_000_000, transcendentals=0
    )


def in_hbm(value):
    return pltpu.with_memory_space_constraint(value, pltpu.HBM)


def merge_rows(block):
    pieces, rows, width = block.shape
    if rows % 16 == 0:
        return block.reshape(pieces * rows, width)
    return block.astype(jnp.float32).reshape(pieces * rows, width).astype(jnp.bfloat16)


def inverse_of(row_values):
    return lax.rsqrt(jnp.mean(row_values * row_values, axis=-1, keepdims=True) + EPSILON)


def encode_kernel(slots, rows_ref, gain_ref, up_ref, down_ref, *refs):
    enc_ref, used_ref, slope_ref, normed, total = refs[-5:]
    step = pl.program_id(0)
    count, piece, width = used_ref.shape

    @pl.when(step == 0)
    def _():
        for g in range(count):
            used_ref[g] = rows_ref[slots[g]]
        row_values = used_ref[...].astype(jnp.float32).reshape(count * piece, width)
        normed[...] = (row_values * inverse_of(row_values) * gain_ref[...]).astype(jnp.bfloat16)
        total[...] = row_values

    before = dot(normed[...], up_ref[...])
    square = before * before
    bend = jnp.tanh(GELU_RATE * before * (1.0 + GELU_CUBE * square))
    half = 0.5 * (1.0 + bend)
    activity = (before * half).astype(jnp.bfloat16)
    slope = half + 0.5 * before * (1.0 - bend * bend) * (
        GELU_RATE * (1.0 + 3.0 * GELU_CUBE * square)
    )
    slope_ref[...] = slope.astype(slope_ref.dtype)
    total[...] += dot(activity, down_ref[...])

    @pl.when(step == pl.num_programs(0) - 1)
    def _():
        enc_ref[...] = total[...].reshape(count, piece, width).astype(jnp.bfloat16)


def encode_rows(slots, rows, gain, up, down, after):
    count = slots.shape[0]
    piece, width = rows.shape[1:]
    hidden = up.shape[1]
    chunk = hidden // 2
    whole = lambda *shape: pl.BlockSpec(shape, lambda f, s: (0,) * len(shape))
    return pl.pallas_call(
        encode_kernel,
        grid_spec=pltpu.PrefetchScalarGridSpec(
            num_scalar_prefetch=1,
            grid=(hidden // chunk,),
            in_specs=[
                whole(*rows.shape),
                whole(1, width),
                pl.BlockSpec((width, chunk), lambda f, s: (0, f)),
                pl.BlockSpec((chunk, width), lambda f, s: (f, 0)),
            ]
            + [pl.BlockSpec(memory_space=pl.ANY)] * len(after),
            out_specs=[
                whole(count, piece, width),
                whole(count, piece, width),
                pl.BlockSpec((count * piece, chunk), lambda f, s: (0, f)),
            ],
            scratch_shapes=[
                pltpu.VMEM((count * piece, width), jnp.bfloat16),
                pltpu.VMEM((count * piece, width), jnp.float32),
            ],
        ),
        out_shape=[
            pltpu.HBM((count, piece, width), jnp.bfloat16),
            pltpu.HBM((count, piece, width), jnp.bfloat16),
            pltpu.HBM((count * piece, hidden), jnp.bfloat16),
        ],
        compiler_params=pltpu.CompilerParams(vmem_limit_bytes=VMEM_BYTES),
        cost_estimate=pl.CostEstimate(
            flops=4 * count * piece * width * hidden,
            bytes_accessed=2 * rows.size + 4 * width * hidden + 8 * count * piece * width,
            transcendentals=count * piece * hidden,
        ),
    )(slots, rows, gain, up, in_hbm(down), *after)


def back_kernel(slots, grad_ref, used_ref, slope_ref, gain_ref, up_ref, down_ref, *refs):
    out_ref, total = refs[-2:]
    step = pl.program_id(0)
    count, piece, width = used_ref.shape
    grads = merge_rows(grad_ref[...])

    @pl.when(step == 0)
    def _():
        out_ref[...] = jnp.zeros_like(out_ref)
        total[...] = jnp.zeros_like(total)

    activity_grad = dot_nt(grads, down_ref[...])
    before_grad = (activity_grad * slope_ref[...]).astype(jnp.bfloat16)
    total[...] += dot_nt(before_grad, up_ref[...])

    @pl.when(step == pl.num_programs(0) - 1)
    def _():
        row_values = used_ref[...].astype(jnp.float32).reshape(count * piece, width)
        inverse = inverse_of(row_values)
        scaled = gain_ref[...] * total[...]
        result = (
            grads.astype(jnp.float32)
            + inverse * scaled
            - row_values
            * (inverse * inverse * inverse)
            * jnp.mean(row_values * scaled, axis=-1, keepdims=True)
        )
        result = result.reshape(count, piece, width).astype(jnp.bfloat16)
        for g in range(count):
            out_ref[slots[g]] = result[g]


def encode_back(slots, grads, used, slope, gain, up, down, slot_count, after):
    count, piece, width = used.shape
    hidden = up.shape[1]
    chunk = hidden // 2
    whole = lambda *shape: pl.BlockSpec(shape, lambda f, s: (0,) * len(shape))
    return pl.pallas_call(
        back_kernel,
        grid_spec=pltpu.PrefetchScalarGridSpec(
            num_scalar_prefetch=1,
            grid=(hidden // chunk,),
            in_specs=[
                whole(count, piece, width),
                whole(count, piece, width),
                pl.BlockSpec((count * piece, chunk), lambda f, s: (0, f)),
                whole(1, width),
                pl.BlockSpec((width, chunk), lambda f, s: (0, f)),
                pl.BlockSpec((chunk, width), lambda f, s: (f, 0)),
            ]
            + [pl.BlockSpec(memory_space=pl.ANY)] * len(after),
            out_specs=whole(slot_count, piece, width),
            scratch_shapes=[pltpu.VMEM((count * piece, width), jnp.float32)],
        ),
        out_shape=pltpu.HBM((slot_count, piece, width), jnp.bfloat16),
        compiler_params=pltpu.CompilerParams(vmem_limit_bytes=VMEM_BYTES),
        cost_estimate=pl.CostEstimate(
            flops=4 * count * piece * width * hidden,
            bytes_accessed=4 * width * hidden + 8 * count * piece * width + 2 * count * piece * hidden,
            transcendentals=0,
        ),
    )(slots, grads, in_hbm(used), in_hbm(slope), gain, up, in_hbm(down), *after)


def attend_kernel(kinds, lines, last, plan, *refs):
    refs = list(refs)
    take = lambda count: [refs.pop(0) for _ in range(count)]
    steps = len(kinds)
    own_enc, other_enc = take(2)
    token_refs = (take(2), take(2))
    weight_refs = [take({"columns": 2, "rows": lines}[kind]) for kind in kinds]
    if last:
        (back_in,) = take(1)
        take(4)
    out_refs = (take(2), take(2))
    back_refs = take(2 if last else 1)
    grad_halves = take(2)
    rows, turned, rows_t, back, weight = refs
    step = pl.program_id(0)
    shares, mine, piece, width = own_enc.shape
    span = shares * piece
    scale = 1.0 / math.sqrt(HD)
    part_rows, columns = width // lines, weight.shape[1] // 2

    @pl.when(step == 0)
    def _():
        for s in range(2 * mine):
            source = own_enc if s < mine else other_enc
            rows[s * span : (s + 1) * span, :] = merge_rows(source[:, s % mine])
        turned[...] = rows[...].T
        for i in range(lines):
            start = pl.multiple_of(plan[steps + i] * part_rows, 16)
            rows_t[i * part_rows : (i + 1) * part_rows, :] = turned[pl.ds(start, part_rows), :]
        back[...] = back_in[...].astype(jnp.float32) if last else jnp.zeros_like(back)

    for shard, (kind, found) in enumerate(zip(kinds, weight_refs)):

        @pl.when(step == shard)
        def _(kind=kind, found=found):
            if kind == "columns":
                weight[:, :columns] = found[0][...]
                weight[:, columns:] = found[1][...]
            else:
                for i in range(lines):
                    start = pl.multiple_of(plan[steps + i] * part_rows, 16)
                    weight[pl.ds(start, part_rows), :] = found[i][...]

    both = dot(rows[...], weight[...]).astype(jnp.bfloat16)
    pairs = [(s, h) for s in range(2 * mine) for h in range(columns // HD)]

    def tokens_of(s, h):
        tokens = slice((s % mine) * STRETCH, (s % mine + 1) * STRETCH)
        return s // mine, tokens, slice(h * HD, (h + 1) * HD)

    def token_block(kind, s, h):
        side, tokens, cols = tokens_of(s, h)
        return token_refs[side][kind][tokens, cols]

    query = [token_block(0, s, h) for s, h in pairs]
    grad = [token_block(1, s, h) for s, h in pairs]
    key = [both[s * span : (s + 1) * span, h * HD : (h + 1) * HD] for s, h in pairs]
    value = [
        both[s * span : (s + 1) * span, columns + h * HD : columns + (h + 1) * HD] for s, h in pairs
    ]
    count = range(len(pairs))
    scores = jnp.concatenate([dot_nt(query[i], key[i]) for i in count], axis=0)
    prob_grad = jnp.concatenate([dot_nt(grad[i], value[i]) for i in count], axis=0)
    exponent = jnp.exp(scores * scale)
    weights = exponent * (1.0 / jnp.sum(exponent, axis=-1, keepdims=True))
    mean_grad = jnp.sum(weights * prob_grad, axis=-1, keepdims=True)
    probabilities = weights.astype(jnp.bfloat16)
    score_grad = (weights * (prob_grad - mean_grad) * scale).astype(jnp.bfloat16)
    prob = [probabilities[i * STRETCH : (i + 1) * STRETCH] for i in count]
    score = [score_grad[i * STRETCH : (i + 1) * STRETCH] for i in count]
    for i, (s, h) in enumerate(pairs):
        side, tokens, cols = tokens_of(s, h)
        out_refs[side][0][tokens, cols] = dot(prob[i], value[i]).astype(jnp.bfloat16)
        out_refs[side][1][tokens, cols] = dot(score[i], key[i]).astype(jnp.bfloat16)
    key_grad = [dot_tn(score[i], query[i]).astype(jnp.bfloat16) for i in count]
    value_grad = [dot_tn(prob[i], grad[i]).astype(jnp.bfloat16) for i in count]
    heads = columns // HD
    both_grad = jnp.concatenate(
        [
            jnp.concatenate(
                key_grad[s * heads : (s + 1) * heads] + value_grad[s * heads : (s + 1) * heads], axis=1
            )
            for s in range(2 * mine)
        ],
        axis=0,
    )
    part_grads = dot(rows_t[...], both_grad).astype(jnp.bfloat16)
    for i in range(lines):
        grad_halves[2 * i // lines][i % (lines // 2), 0] = part_grads[
            i * part_rows : (i + 1) * part_rows
        ]
    back[...] += dot_nt(both_grad, weight[...])

    @pl.when(step == steps - 1)
    def _():
        if not last:
            back_refs[0][...] = back[...].astype(jnp.bfloat16)
        else:
            for s in range(2 * mine):
                block = back[s * span : (s + 1) * span, :].reshape(shares, piece, width)
                back_refs[s // mine][:, s % mine] = block.astype(jnp.bfloat16)


def attend(plan, lines, own_enc, other_enc, token_arrays, shards, earlier=None):
    last = earlier is not None
    steps = len(shards)
    kinds, arrays = [kind for kind, _ in shards], sum([found for _, found in shards], [])
    shares, mine, piece, width = own_enc.shape
    tokens, all_columns = token_arrays[0].shape
    columns = all_columns // shares
    part_rows = width // lines
    span = shares * piece
    all_rows = 2 * mine * span
    whole = lambda *shape: pl.BlockSpec(shape, lambda j, p: (0,) * len(shape))
    token_spec = pl.BlockSpec((tokens, columns), lambda j, p: (0, p[j]))
    enc_spec = whole(*own_enc.shape)
    out = functools.partial(jax.ShapeDtypeStruct, dtype=jnp.bfloat16)
    operands = [plan, own_enc, other_enc, *map(in_hbm, token_arrays), *arrays]
    in_specs = [enc_spec] * 2 + [token_spec] * 4 + [whole(*value.shape) for value in arrays]
    back_shapes, aliases = [out((all_rows, width))], {}
    if last:
        aliases = {len(operands) + 1 + i: i for i in range(4)}
        operands += [earlier[4], *map(in_hbm, earlier[:4])]
        in_specs += [whole(all_rows, width)] + [pl.BlockSpec(memory_space=pl.ANY)] * 4
        back_shapes = [out(own_enc.shape)] * 2
    return pl.pallas_call(
        functools.partial(attend_kernel, kinds, lines, last),
        grid_spec=pltpu.PrefetchScalarGridSpec(
            num_scalar_prefetch=1,
            grid=(steps,),
            in_specs=in_specs,
            out_specs=[token_spec] * 4
            + [whole(*shape.shape) for shape in back_shapes]
            + [pl.BlockSpec((lines // 2, 1, part_rows, 2 * columns), lambda j, p: (0, j, 0, 0))] * 2,
            scratch_shapes=[
                pltpu.VMEM((all_rows, width), jnp.bfloat16),
                pltpu.VMEM((width, all_rows), jnp.bfloat16),
                pltpu.VMEM((width, all_rows), jnp.bfloat16),
                pltpu.VMEM((all_rows, width), jnp.float32),
                pltpu.VMEM((width, 2 * columns), jnp.bfloat16),
            ],
        ),
        out_shape=[pltpu.HBM((tokens, all_columns), jnp.bfloat16)] * 4
        + back_shapes
        + [pltpu.HBM((lines // 2, steps, part_rows, 2 * columns), jnp.bfloat16)] * 2,
        input_output_aliases=aliases,
        compiler_params=pltpu.CompilerParams(vmem_limit_bytes=VMEM_BYTES),
        cost_estimate=pl.CostEstimate(
            flops=12 * all_rows * width * steps * columns,
            bytes_accessed=8 * width * steps * columns + 8 * own_enc.size + 16 * tokens * steps * columns,
            transcendentals=2 * mine * STRETCH * span * steps * columns // HD,
        ),
    )(*operands)


def sum_kernel(count, sizes, *refs):
    terms, outs = refs[:count], refs[len(refs) - len(sizes) :]
    block = 0
    for size, out in zip(sizes, outs):
        for i in range(size):
            total = terms[0][block].astype(jnp.float32)
            for term in terms[1:]:
                total = total + term[block].astype(jnp.float32)
            out[i] = total.astype(jnp.bfloat16)
            block += 1


def sum_blocks(terms, sizes, after=(), to_hbm=False):
    blocks, rows, columns = terms[0].shape
    tiles = 2 if rows % 32 == 0 else 1
    spec = lambda size: pl.BlockSpec((size, rows // tiles, columns), lambda i: (0, i, 0))
    return pl.pallas_call(
        functools.partial(sum_kernel, len(terms), sizes),
        grid=(tiles,),
        in_specs=[spec(blocks)] * len(terms) + [pl.BlockSpec(memory_space=pl.ANY)] * len(after),
        out_specs=[spec(size) for size in sizes],
        out_shape=[
            (pltpu.HBM if to_hbm else jax.ShapeDtypeStruct)((size, rows, columns), jnp.bfloat16)
            for size in sizes
        ],
        compiler_params=pltpu.CompilerParams(vmem_limit_bytes=SMALL_VMEM_BYTES),
        cost_estimate=pl.CostEstimate(
            flops=len(terms) * blocks * rows * columns,
            bytes_accessed=2 * (len(terms) + 1) * blocks * rows * columns,
            transcendentals=0,
        ),
    )(*terms, *after)


def copy_kernel(plan, *refs):
    out = refs[-1]
    for i in range(plan.shape[0]):
        out[i] = plan[i]


def copy_plan(plan, others):
    scalars = pl.BlockSpec(memory_space=pltpu.SMEM)
    return pl.pallas_call(
        copy_kernel,
        in_specs=[scalars] + [pl.BlockSpec(memory_space=pl.ANY)] * len(others),
        out_specs=scalars,
        out_shape=jax.ShapeDtypeStruct(plan.shape, plan.dtype),
        compiler_params=pltpu.CompilerParams(vmem_limit_bytes=SMALL_VMEM_BYTES),
        cost_estimate=stated(4),
    )(plan, *others)


def join_kernel(plan, *refs):
    parts, outs = refs[:-2], refs[-2:]
    part_rows, columns = parts[0].shape[0], outs[0].shape[1]
    for i, part in enumerate(parts):
        start = pl.multiple_of(plan[i] * part_rows, 16)
        for k, out in enumerate(outs):
            out[pl.ds(start, part_rows), :] = part[:, k * columns : (k + 1) * columns].astype(out.dtype)


def join_grads(plan, parts):
    part_rows, columns = parts[0].shape
    width = part_rows * len(parts)
    whole = lambda *shape: pl.BlockSpec(shape, lambda j, p: (0,) * len(shape))
    return pl.pallas_call(
        join_kernel,
        grid_spec=pltpu.PrefetchScalarGridSpec(
            num_scalar_prefetch=1,
            grid=(1,),
            in_specs=[whole(part_rows, columns)] * len(parts),
            out_specs=[whole(width, columns // 2)] * 2,
        ),
        out_shape=[jax.ShapeDtypeStruct((width, columns // 2), jnp.float32)] * 2,
        compiler_params=pltpu.CompilerParams(vmem_limit_bytes=SMALL_VMEM_BYTES),
        cost_estimate=stated(8),
    )(plan, *parts)


def swap_cores(value):
    return lax.ppermute(value, "core", [(0, 1), (1, 0)])


def swap_chips(value, shift):
    return lax.ppermute(value, "z", [(z, z ^ shift) for z in range(lax.axis_size("z"))])


def line_bit(core, stage, stages):
    return 1 << stage if core == 0 else 1 << (stages - 1 - stage)


def swap_lines(value, stage, stages):
    lines = lax.axis_size("line")
    pairs = [
        (line * 2 + core, (line ^ line_bit(core, stage, stages)) * 2 + core)
        for line in range(lines)
        for core in range(2)
    ]
    return lax.ppermute(value, ("line", "core"), pairs)


def gather_lines(value, stages):
    found = [value]
    for stage in range(stages):
        found = found + [swap_lines(item, stage, stages) for item in found]
    return found


def on_device(
    queries,
    attended_grad,
    neighbour_pool,
    stretch_slot,
    enc_gain,
    enc_up,
    enc_down,
    key_weight,
    value_weight,
):
    chips, lines = lax.axis_size("z"), lax.axis_size("line")
    stages = lines.bit_length() - 1
    groups = 2 * chips
    core, chip, line = lax.axis_index("core"), lax.axis_index("z"), lax.axis_index("line")
    tokens, all_columns = queries.shape[1:]
    mine = tokens // STRETCH
    holding, span, width = neighbour_pool.shape[1:]
    piece = span // groups
    columns = key_weight.shape[1]
    slots = stretch_slot[0]
    gain = enc_gain.reshape(1, width)

    offsets = [
        [sum(line_bit(c, s, stages) for s in range(stages) if i >> s & 1) for i in range(lines)]
        for c in range(2)
    ]
    part_lines = line ^ jnp.where(
        core == 0, jnp.array(offsets[0], jnp.int32), jnp.array(offsets[1], jnp.int32)
    )
    part_lines = part_lines.astype(jnp.int32)

    part_rows = width // lines
    part = jnp.concatenate(
        [
            lax.dynamic_slice_in_dim(weight, line * part_rows, part_rows, 0)
            for weight in (key_weight, value_weight)
        ],
        axis=1,
    )
    odd, even = range(1, chips, 2), range(2, chips, 2)
    part = {0: part}
    shift = chips // 2
    while shift > 1:
        part |= {s | shift: swap_chips(value, shift) for s, value in part.items()}
        shift //= 2
    part[1] = swap_chips(part[0], 1)

    pieces = neighbour_pool[0].reshape(holding, groups, piece, width).transpose(1, 0, 2, 3)
    received = lax.all_to_all(pieces, SEQ, split_axis=0, concat_axis=0, tiled=True)
    received = received.reshape(groups * holding, piece, width)

    token_arrays = [queries[0], attended_grad[0]]
    token_arrays += [swap_cores(value) for value in token_arrays]

    encoded, used, slope = encode_rows(slots, received, gain, enc_up, enc_down, [])
    encoded, part = lax.optimization_barrier((encoded, part))
    part |= {s | 1: swap_chips(part[s], 1) for s in even}
    own_enc = lax.all_to_all(
        encoded.reshape(groups, mine, piece, width), SEQ, split_axis=0, concat_axis=0, tiled=True
    )
    shards = {0: ("columns", [in_hbm(key_weight), in_hbm(value_weight)])}
    for shift in range(1, chips):
        shards[shift] = ("rows", gather_lines(part[shift], stages))
    other_enc = swap_cores(own_enc)

    steps = ([0, *even], [*odd])
    plans = [
        jnp.concatenate([jnp.stack([(chip ^ shift) * 2 + core for shift in shifts]), part_lines])
        for shifts in steps
    ]
    early = [value for shift in (1, *even) for value in shards[shift][1][lines // 2 :]]
    plans[0] = copy_plan(plans[0], early)
    parted = [[shards[shift] for shift in shifts] for shifts in steps]
    first = attend(plans[0], lines, own_enc, other_enc, token_arrays, parted[0])
    last = attend(plans[1], lines, own_enc, other_enc, token_arrays, parted[1], first[:5])
    outs, own_back, other_back = last[:4], last[4], last[5]

    rows = groups * mine * piece
    (back,) = sum_blocks(
        [own_back.reshape(1, rows, width), swap_cores(other_back).reshape(1, rows, width)],
        (1,),
        to_hbm=True,
    )
    split_rows = lax.all_to_all(
        back.reshape(groups, mine, piece, width), SEQ, split_axis=0, concat_axis=0, tiled=True
    )

    count = chips // 2
    first_halves = [first[5], swap_lines(first[6], stages - 1, stages)]
    last_halves = [last[6], swap_lines(last[7], stages - 1, stages)]
    after = [in_hbm(back)]
    for stage in reversed(range(stages)):
        size = first_halves[0].size // (part_rows * 2 * columns)
        sizes = (size // 2, size // 2) if stage else (1,) * count
        flat = lambda halves: [value.reshape(size, part_rows, 2 * columns) for value in halves]
        first_flat, last_flat = flat(first_halves), flat(last_halves)
        if stage == stages - 1:
            first_flat[0], last_flat[0] = in_hbm(first_flat[0]), in_hbm(last_flat[0])
        first_sums = sum_blocks(first_flat, sizes, after)
        last_sums = sum_blocks(last_flat, sizes, [first_sums[0]])
        after = [last_sums[0]]
        if stage:
            first_halves = [first_sums[0], swap_lines(first_sums[1], stage - 1, stages)]
            last_halves = [last_sums[0], swap_lines(last_sums[1], stage - 1, stages)]
    terms = {0: first_sums[0]}
    terms |= {shift: swap_chips(value, shift) for value, shift in zip(first_sums[1:], even)}
    terms |= {shift: swap_chips(value, shift) for value, shift in zip(last_sums, odd)}
    placed = encode_back(
        slots,
        split_rows.reshape(groups * mine, piece, width),
        used,
        slope,
        gain,
        enc_up,
        enc_down,
        groups * holding,
        [terms[shift] for shift in even],
    )
    (share,) = sum_blocks([*terms.values()], (1,), [in_hbm(placed)])
    share = share[0]
    if lax.axis_size("far") > 1:
        share = lax.psum(share, "far")
    weight_grads = join_grads(part_lines, gather_lines(share, stages))

    returned = lax.all_to_all(
        placed.reshape(groups, holding, piece, width), SEQ, split_axis=0, concat_axis=0, tiled=True
    )
    pool_grad = returned.transpose(1, 0, 2, 3).reshape(1, holding, span, width)

    is_own = (lax.broadcasted_iota(jnp.int32, (1, all_columns), 1) // columns) % 2 == core
    outs = [jnp.where(is_own, outs[i], swap_cores(outs[2 + i]))[None] for i in range(2)]
    return outs[0], outs[1], pool_grad, weight_grads[0], weight_grads[1]


def solution(mesh):
    dp, seq = mesh.shape["dp"], mesh.shape["seq"]
    lines = 4 if dp % 4 == 0 else dp
    fine = Mesh(
        mesh.devices.reshape(dp // lines, lines, seq // 2, 2), ("far", "line", "z", "core")
    )
    dp_axes = ("far", "line")
    return jax.shard_map(
        on_device,
        mesh=fine,
        in_specs=(
            P(dp_axes, SEQ, None),
            P(dp_axes, SEQ, None),
            P(dp_axes, SEQ, None, None),
            P(dp_axes, None),
            P(),
            P(),
            P(),
            P(None, SEQ),
            P(None, SEQ),
        ),
        out_specs=(
            P(dp_axes, SEQ, None),
            P(dp_axes, SEQ, None),
            P(dp_axes, SEQ, None, None),
            P(None, SEQ),
            P(None, SEQ),
        ),
        check_vma=False,
    )
```

```python
import functools
import math

import jax
import jax.numpy as jnp
from jax import lax
from jax.experimental import pallas as pl
from jax.experimental.pallas import tpu as pltpu
from jax.sharding import Mesh, PartitionSpec as P

STRETCH = 64
HD = 128
EPSILON = 1e-06
GELU_RATE = math.sqrt(2.0 / math.pi)
GELU_CUBE = 0.044715
VMEM_BYTES = 28 * 1024 * 1024
SMALL_VMEM_BYTES = 12 * 1024 * 1024
SEQ = ("z", "core")


def dot(left, right):
    return jnp.dot(left, right, preferred_element_type=jnp.float32)


def dot_nt(left, right):
    return lax.dot_general(left, right, (((1,), (1,)), ((), ())), preferred_element_type=jnp.float32)


def dot_tn(left, right):
    return lax.dot_general(left, right, (((0,), (0,)), ((), ())), preferred_element_type=jnp.float32)


def stated(microseconds):
    return pl.CostEstimate(
        flops=microseconds * 1_000_000_000, bytes_accessed=microseconds * 3_000_000, transcendentals=0
    )


def in_hbm(value):
    return pltpu.with_memory_space_constraint(value, pltpu.HBM)


def merge_rows(block):
    pieces, rows, width = block.shape
    if rows % 16 == 0:
        return block.reshape(pieces * rows, width)
    return block.astype(jnp.float32).reshape(pieces * rows, width).astype(jnp.bfloat16)


def inverse_of(row_values):
    return lax.rsqrt(jnp.mean(row_values * row_values, axis=-1, keepdims=True) + EPSILON)


def encode_kernel(slots, rows_ref, gain_ref, up_ref, down_ref, *refs):
    enc_ref, used_ref, slope_ref, normed, total = refs[-5:]
    step = pl.program_id(0)
    count, piece, width = used_ref.shape

    @pl.when(step == 0)
    def _():
        for g in range(count):
            used_ref[g] = rows_ref[slots[g]]
        row_values = used_ref[...].astype(jnp.float32).reshape(count * piece, width)
        normed[...] = (row_values * inverse_of(row_values) * gain_ref[...]).astype(jnp.bfloat16)
        total[...] = row_values

    before = dot(normed[...], up_ref[...])
    square = before * before
    bend = jnp.tanh(before * (GELU_RATE + GELU_RATE * GELU_CUBE * square))
    half = 0.5 + 0.5 * bend
    activity = before * half
    slope = half + activity * (1.0 - bend) * (GELU_RATE + 3.0 * GELU_RATE * GELU_CUBE * square)
    slope_ref[...] = slope.astype(slope_ref.dtype)
    total[...] += dot(activity.astype(jnp.bfloat16), down_ref[...])

    @pl.when(step == pl.num_programs(0) - 1)
    def _():
        enc_ref[...] = total[...].reshape(count, piece, width).astype(jnp.bfloat16)


def encode_rows(slots, rows, gain, up, down, after):
    count = slots.shape[0]
    piece, width = rows.shape[1:]
    hidden = up.shape[1]
    chunk = hidden // 2
    whole = lambda *shape: pl.BlockSpec(shape, lambda f, s: (0,) * len(shape))
    return pl.pallas_call(
        encode_kernel,
        grid_spec=pltpu.PrefetchScalarGridSpec(
            num_scalar_prefetch=1,
            grid=(hidden // chunk,),
            in_specs=[
                whole(*rows.shape),
                whole(1, width),
                pl.BlockSpec((width, chunk), lambda f, s: (0, f)),
                pl.BlockSpec((chunk, width), lambda f, s: (f, 0)),
            ]
            + [pl.BlockSpec(memory_space=pl.ANY)] * len(after),
            out_specs=[
                whole(count, piece, width),
                whole(count, piece, width),
                pl.BlockSpec((count * piece, chunk), lambda f, s: (0, f)),
            ],
            scratch_shapes=[
                pltpu.VMEM((count * piece, width), jnp.bfloat16),
                pltpu.VMEM((count * piece, width), jnp.float32),
            ],
        ),
        out_shape=[
            pltpu.HBM((count, piece, width), jnp.bfloat16),
            pltpu.HBM((count, piece, width), jnp.bfloat16),
            pltpu.HBM((count * piece, hidden), jnp.bfloat16),
        ],
        compiler_params=pltpu.CompilerParams(vmem_limit_bytes=VMEM_BYTES),
        cost_estimate=pl.CostEstimate(
            flops=4 * count * piece * width * hidden,
            bytes_accessed=2 * rows.size + 4 * width * hidden + 8 * count * piece * width,
            transcendentals=count * piece * hidden,
        ),
    )(slots, rows, gain, up, in_hbm(down), *after)


def back_kernel(slots, grad_ref, used_ref, slope_ref, gain_ref, up_ref, down_ref, *refs):
    out_ref, total = refs[-2:]
    step = pl.program_id(0)
    count, piece, width = used_ref.shape
    grads = merge_rows(grad_ref[...])

    @pl.when(step == 0)
    def _():
        out_ref[...] = jnp.zeros_like(out_ref)
        total[...] = jnp.zeros_like(total)

    activity_grad = dot_nt(grads, down_ref[...])
    before_grad = (activity_grad * slope_ref[...]).astype(jnp.bfloat16)
    total[...] += dot_nt(before_grad, up_ref[...])

    @pl.when(step == pl.num_programs(0) - 1)
    def _():
        row_values = used_ref[...].astype(jnp.float32).reshape(count * piece, width)
        inverse = inverse_of(row_values)
        scaled = gain_ref[...] * total[...]
        result = (
            grads.astype(jnp.float32)
            + inverse * scaled
            - row_values
            * (inverse * inverse * inverse)
            * jnp.mean(row_values * scaled, axis=-1, keepdims=True)
        )
        result = result.reshape(count, piece, width).astype(jnp.bfloat16)
        for g in range(count):
            out_ref[slots[g]] = result[g]


def encode_back(slots, grads, used, slope, gain, up, down, slot_count, after):
    count, piece, width = used.shape
    hidden = up.shape[1]
    chunk = hidden // 2
    whole = lambda *shape: pl.BlockSpec(shape, lambda f, s: (0,) * len(shape))
    return pl.pallas_call(
        back_kernel,
        grid_spec=pltpu.PrefetchScalarGridSpec(
            num_scalar_prefetch=1,
            grid=(hidden // chunk,),
            in_specs=[
                whole(count, piece, width),
                whole(count, piece, width),
                pl.BlockSpec((count * piece, chunk), lambda f, s: (0, f)),
                whole(1, width),
                pl.BlockSpec((width, chunk), lambda f, s: (0, f)),
                pl.BlockSpec((chunk, width), lambda f, s: (f, 0)),
            ]
            + [pl.BlockSpec(memory_space=pl.ANY)] * len(after),
            out_specs=whole(slot_count, piece, width),
            scratch_shapes=[pltpu.VMEM((count * piece, width), jnp.float32)],
        ),
        out_shape=pltpu.HBM((slot_count, piece, width), jnp.bfloat16),
        compiler_params=pltpu.CompilerParams(vmem_limit_bytes=VMEM_BYTES),
        cost_estimate=pl.CostEstimate(
            flops=4 * count * piece * width * hidden,
            bytes_accessed=4 * width * hidden + 8 * count * piece * width + 2 * count * piece * hidden,
            transcendentals=0,
        ),
    )(slots, grads, in_hbm(used), in_hbm(slope), gain, up, in_hbm(down), *after)


def attend_kernel(kinds, lines, last, plan, *refs):
    refs = list(refs)
    take = lambda count: [refs.pop(0) for _ in range(count)]
    steps = len(kinds)
    own_enc, other_enc = take(2)
    token_refs = (take(2), take(2))
    weight_refs = [take({"columns": 2, "rows": lines}[kind]) for kind in kinds]
    if last:
        (back_in,) = take(1)
        take(4)
    else:
        take(1)
    out_refs = (take(2), take(2))
    back_refs = take(2 if last else 1)
    grad_halves = take(2)
    rows, rows_t, back, weight = refs
    step = pl.program_id(0)
    shares, mine, piece, width = own_enc.shape
    span = shares * piece
    scale = 1.0 / math.sqrt(HD)
    part_rows, columns = width // lines, weight.shape[1] // 2

    @pl.when(step == 0)
    def _():
        for s in range(2 * mine):
            source = own_enc if s < mine else other_enc
            rows[s * span : (s + 1) * span, :] = merge_rows(source[:, s % mine])
        rows_t[...] = rows[...].T
        back[...] = back_in[...].astype(jnp.float32) if last else jnp.zeros_like(back)

    for shard, (kind, found) in enumerate(zip(kinds, weight_refs)):

        @pl.when(step == shard)
        def _(kind=kind, found=found):
            if kind == "columns":
                weight[:, :columns] = found[0][...]
                weight[:, columns:] = found[1][...]
            else:
                for i in range(lines):
                    start = pl.multiple_of(plan[steps + i] * part_rows, 16)
                    weight[pl.ds(start, part_rows), :] = found[i][...]

    both = dot(rows[...], weight[...]).astype(jnp.bfloat16)
    pairs = [(s, h) for s in range(2 * mine) for h in range(columns // HD)]

    def tokens_of(s, h):
        tokens = slice((s % mine) * STRETCH, (s % mine + 1) * STRETCH)
        return s // mine, tokens, slice(h * HD, (h + 1) * HD)

    def token_block(kind, s, h):
        side, tokens, cols = tokens_of(s, h)
        return token_refs[side][kind][tokens, cols]

    query = [token_block(0, s, h) for s, h in pairs]
    grad = [token_block(1, s, h) for s, h in pairs]
    key = [both[s * span : (s + 1) * span, h * HD : (h + 1) * HD] for s, h in pairs]
    value = [
        both[s * span : (s + 1) * span, columns + h * HD : columns + (h + 1) * HD] for s, h in pairs
    ]
    count = range(len(pairs))
    scores = jnp.concatenate([dot_nt(query[i], key[i]) for i in count], axis=0)
    prob_grad = jnp.concatenate([dot_nt(grad[i], value[i]) for i in count], axis=0)
    exponent = jnp.exp(scores * scale)
    weights = exponent * (1.0 / jnp.sum(exponent, axis=-1, keepdims=True))
    mean_grad = jnp.sum(weights * prob_grad, axis=-1, keepdims=True)
    probabilities = weights.astype(jnp.bfloat16)
    score_grad = (weights * (prob_grad - mean_grad) * scale).astype(jnp.bfloat16)
    prob = [probabilities[i * STRETCH : (i + 1) * STRETCH] for i in count]
    score = [score_grad[i * STRETCH : (i + 1) * STRETCH] for i in count]
    for i, (s, h) in enumerate(pairs):
        side, tokens, cols = tokens_of(s, h)
        out_refs[side][0][tokens, cols] = dot(prob[i], value[i]).astype(jnp.bfloat16)
        out_refs[side][1][tokens, cols] = dot(score[i], key[i]).astype(jnp.bfloat16)
    key_grad = [dot_tn(score[i], query[i]).astype(jnp.bfloat16) for i in count]
    value_grad = [dot_tn(prob[i], grad[i]).astype(jnp.bfloat16) for i in count]
    heads = columns // HD
    both_grad = jnp.concatenate(
        [
            jnp.concatenate(
                key_grad[s * heads : (s + 1) * heads] + value_grad[s * heads : (s + 1) * heads], axis=1
            )
            for s in range(2 * mine)
        ],
        axis=0,
    )
    for i in range(lines):
        start = pl.multiple_of(plan[steps + i] * part_rows, 16)
        part_grad = dot(rows_t[pl.ds(start, part_rows), :], both_grad).astype(jnp.bfloat16)
        grad_halves[2 * i // lines][i % (lines // 2), 0] = part_grad
    back[...] += dot_nt(both_grad, weight[...])

    @pl.when(step == steps - 1)
    def _():
        if not last:
            back_refs[0][...] = back[...].astype(jnp.bfloat16)
        else:
            for s in range(2 * mine):
                block = back[s * span : (s + 1) * span, :].reshape(shares, piece, width)
                back_refs[s // mine][:, s % mine] = block.astype(jnp.bfloat16)


def attend(plan, lines, own_enc, other_enc, token_arrays, shards, earlier=None, token=None):
    last = earlier is not None
    steps = len(shards)
    kinds, arrays = [kind for kind, _ in shards], sum([found for _, found in shards], [])
    shares, mine, piece, width = own_enc.shape
    tokens, all_columns = token_arrays[0].shape
    columns = all_columns // shares
    part_rows = width // lines
    span = shares * piece
    all_rows = 2 * mine * span
    whole = lambda *shape: pl.BlockSpec(shape, lambda j, p: (0,) * len(shape))
    token_spec = pl.BlockSpec((tokens, columns), lambda j, p: (0, p[j]))
    enc_spec = whole(*own_enc.shape)
    out = functools.partial(jax.ShapeDtypeStruct, dtype=jnp.bfloat16)
    operands = [plan, own_enc, other_enc, *map(in_hbm, token_arrays), *arrays]
    in_specs = [enc_spec] * 2 + [token_spec] * 4 + [whole(*value.shape) for value in arrays]
    if token is not None:
        operands.append(token)
        in_specs.append(pl.BlockSpec(memory_space=pl.ANY))
    back_shapes, aliases = [out((all_rows, width))], {}
    if last:
        aliases = {len(operands) + 1 + i: i for i in range(4)}
        operands += [earlier[4], *map(in_hbm, earlier[:4])]
        in_specs += [whole(all_rows, width)] + [pl.BlockSpec(memory_space=pl.ANY)] * 4
        back_shapes = [out(own_enc.shape)] * 2
    return pl.pallas_call(
        functools.partial(attend_kernel, kinds, lines, last),
        grid_spec=pltpu.PrefetchScalarGridSpec(
            num_scalar_prefetch=1,
            grid=(steps,),
            in_specs=in_specs,
            out_specs=[token_spec] * 4
            + [whole(*shape.shape) for shape in back_shapes]
            + [pl.BlockSpec((lines // 2, 1, part_rows, 2 * columns), lambda j, p: (0, j, 0, 0))] * 2,
            scratch_shapes=[
                pltpu.VMEM((all_rows, width), jnp.bfloat16),
                pltpu.VMEM((width, all_rows), jnp.bfloat16),
                pltpu.VMEM((all_rows, width), jnp.float32),
                pltpu.VMEM((width, 2 * columns), jnp.bfloat16),
            ],
        ),
        out_shape=[pltpu.HBM((tokens, all_columns), jnp.bfloat16)] * 4
        + back_shapes
        + [pltpu.HBM((lines // 2, steps, part_rows, 2 * columns), jnp.bfloat16)] * 2,
        input_output_aliases=aliases,
        compiler_params=pltpu.CompilerParams(vmem_limit_bytes=VMEM_BYTES),
        cost_estimate=pl.CostEstimate(
            flops=12 * all_rows * width * steps * columns,
            bytes_accessed=8 * width * steps * columns + 8 * own_enc.size + 16 * tokens * steps * columns,
            transcendentals=2 * mine * STRETCH * span * steps * columns // HD,
        ),
    )(*operands)


def sum_kernel(count, sizes, *refs):
    terms, outs = refs[:count], refs[len(refs) - len(sizes) :]
    block = 0
    for size, out in zip(sizes, outs):
        for i in range(size):
            total = terms[0][block].astype(jnp.float32)
            for term in terms[1:]:
                total = total + term[block].astype(jnp.float32)
            out[i] = total.astype(jnp.bfloat16)
            block += 1


def sum_blocks(terms, sizes, after=(), to_hbm=False):
    blocks, rows, columns = terms[0].shape
    tiles = 2 if rows % 32 == 0 else 1
    spec = lambda size: pl.BlockSpec((size, rows // tiles, columns), lambda i: (0, i, 0))
    return pl.pallas_call(
        functools.partial(sum_kernel, len(terms), sizes),
        grid=(tiles,),
        in_specs=[spec(blocks)] * len(terms) + [pl.BlockSpec(memory_space=pl.ANY)] * len(after),
        out_specs=[spec(size) for size in sizes],
        out_shape=[
            (pltpu.HBM if to_hbm else jax.ShapeDtypeStruct)((size, rows, columns), jnp.bfloat16)
            for size in sizes
        ],
        compiler_params=pltpu.CompilerParams(vmem_limit_bytes=SMALL_VMEM_BYTES),
        cost_estimate=pl.CostEstimate(
            flops=len(terms) * blocks * rows * columns,
            bytes_accessed=2 * (len(terms) + 1) * blocks * rows * columns,
            transcendentals=0,
        ),
    )(*terms, *after)


def token_kernel(*refs):
    refs[-1][...] = jnp.zeros_like(refs[-1])


def token_after(others):
    return pl.pallas_call(
        token_kernel,
        in_specs=[pl.BlockSpec(memory_space=pl.ANY)] * len(others),
        out_specs=pl.BlockSpec(memory_space=pltpu.VMEM),
        out_shape=jax.ShapeDtypeStruct((8, 128), jnp.float32),
        compiler_params=pltpu.CompilerParams(vmem_limit_bytes=SMALL_VMEM_BYTES),
        cost_estimate=stated(4),
    )(*others)


def share_kernel(pool, out, held, read, wrote):
    holding, groups = pool.shape[:2]
    half = groups // 2
    ranges = [pl.ds(part * half, half) for part in range(2)]
    reads = [
        [
            pltpu.make_async_copy(pool.at[slot, shares], held.at[shares, slot], read.at[part, slot])
            for slot in range(holding)
        ]
        for part, shares in enumerate(ranges)
    ]
    writes = [
        pltpu.make_async_copy(held.at[shares], out.at[shares], wrote.at[part])
        for part, shares in enumerate(ranges)
    ]
    for copy in reads[0] + reads[1]:
        copy.start()
    for part in range(2):
        for copy in reads[part]:
            copy.wait()
        writes[part].start()
    for copy in writes:
        copy.wait()


def share_rows(pool):
    holding, groups, piece, width = pool.shape
    shape = (groups, holding, piece, width)
    return pl.pallas_call(
        share_kernel,
        in_specs=[pl.BlockSpec(memory_space=pl.ANY)],
        out_specs=pl.BlockSpec(memory_space=pl.ANY),
        out_shape=pltpu.HBM(shape, pool.dtype),
        scratch_shapes=[
            pltpu.VMEM(shape, pool.dtype),
            pltpu.SemaphoreType.DMA((2, holding)),
            pltpu.SemaphoreType.DMA((2,)),
        ],
        compiler_params=pltpu.CompilerParams(vmem_limit_bytes=SMALL_VMEM_BYTES),
        cost_estimate=pl.CostEstimate(flops=0, bytes_accessed=4 * pool.size, transcendentals=0),
    )(in_hbm(pool))


def join_kernel(plan, *refs):
    parts, outs = refs[:-2], refs[-2:]
    part_rows, columns = parts[0].shape[0], outs[0].shape[1]
    for i, part in enumerate(parts):
        start = pl.multiple_of(plan[i] * part_rows, 16)
        for k, out in enumerate(outs):
            out[pl.ds(start, part_rows), :] = part[:, k * columns : (k + 1) * columns].astype(out.dtype)


def join_grads(plan, parts):
    part_rows, columns = parts[0].shape
    width = part_rows * len(parts)
    whole = lambda *shape: pl.BlockSpec(shape, lambda j, p: (0,) * len(shape))
    return pl.pallas_call(
        join_kernel,
        grid_spec=pltpu.PrefetchScalarGridSpec(
            num_scalar_prefetch=1,
            grid=(1,),
            in_specs=[whole(part_rows, columns)] * len(parts),
            out_specs=[whole(width, columns // 2)] * 2,
        ),
        out_shape=[jax.ShapeDtypeStruct((width, columns // 2), jnp.float32)] * 2,
        compiler_params=pltpu.CompilerParams(vmem_limit_bytes=SMALL_VMEM_BYTES),
        cost_estimate=stated(8),
    )(plan, *parts)


def swap_cores(value):
    return lax.ppermute(value, "core", [(0, 1), (1, 0)])


def swap_chips(value, shift):
    return lax.ppermute(value, "z", [(z, z ^ shift) for z in range(lax.axis_size("z"))])


def line_bit(core, stage, stages):
    return 1 << stage if core == 0 else 1 << (stages - 1 - stage)


def swap_lines(value, stage, stages):
    lines = lax.axis_size("line")
    pairs = [
        (line * 2 + core, (line ^ line_bit(core, stage, stages)) * 2 + core)
        for line in range(lines)
        for core in range(2)
    ]
    return lax.ppermute(value, ("line", "core"), pairs)


def gather_lines(value, stages):
    found = [value]
    for stage in range(stages):
        found = found + [swap_lines(item, stage, stages) for item in found]
    return found


def on_device(
    queries,
    attended_grad,
    neighbour_pool,
    stretch_slot,
    enc_gain,
    enc_up,
    enc_down,
    key_weight,
    value_weight,
):
    chips, lines = lax.axis_size("z"), lax.axis_size("line")
    stages = lines.bit_length() - 1
    groups = 2 * chips
    core, chip, line = lax.axis_index("core"), lax.axis_index("z"), lax.axis_index("line")
    tokens, all_columns = queries.shape[1:]
    mine = tokens // STRETCH
    holding, span, width = neighbour_pool.shape[1:]
    piece = span // groups
    columns = key_weight.shape[1]
    slots = stretch_slot[0]
    gain = enc_gain.reshape(1, width)

    offsets = [
        [sum(line_bit(c, s, stages) for s in range(stages) if i >> s & 1) for i in range(lines)]
        for c in range(2)
    ]
    part_lines = line ^ jnp.where(
        core == 0, jnp.array(offsets[0], jnp.int32), jnp.array(offsets[1], jnp.int32)
    )
    part_lines = part_lines.astype(jnp.int32)

    part_rows = width // lines
    part = jnp.concatenate(
        [
            lax.dynamic_slice_in_dim(weight, line * part_rows, part_rows, 0)
            for weight in (key_weight, value_weight)
        ],
        axis=1,
    )
    odd, even = range(1, chips, 2), range(2, chips, 2)
    part = {0: part}
    shift = chips // 2
    while shift > 1:
        part |= {s | shift: swap_chips(value, shift) for s, value in part.items()}
        shift //= 2
    part[1] = swap_chips(part[0], 1)

    pieces = share_rows(neighbour_pool[0].reshape(holding, groups, piece, width))
    received = lax.all_to_all(pieces, SEQ, split_axis=0, concat_axis=0, tiled=True)
    received = received.reshape(groups * holding, piece, width)

    token_arrays = [queries[0], attended_grad[0]]
    token_arrays += [swap_cores(value) for value in token_arrays]

    encoded, used, slope = encode_rows(slots, received, gain, enc_up, enc_down, [])
    encoded, part = lax.optimization_barrier((encoded, part))
    part |= {s | 1: swap_chips(part[s], 1) for s in even}
    own_enc = lax.all_to_all(
        encoded.reshape(groups, mine, piece, width), SEQ, split_axis=0, concat_axis=0, tiled=True
    )
    shards = {0: ("columns", [in_hbm(key_weight), in_hbm(value_weight)])}
    for shift in range(1, chips):
        shards[shift] = ("rows", gather_lines(part[shift], stages))
    other_enc = swap_cores(own_enc)

    steps = ([0, *even], [*odd])
    plans = [
        jnp.concatenate([jnp.stack([(chip ^ shift) * 2 + core for shift in shifts]), part_lines])
        for shifts in steps
    ]
    early = [value for shift in (1, *even) for value in shards[shift][1][lines // 2 :]]
    token = token_after(early)
    parted = [[shards[shift] for shift in shifts] for shifts in steps]
    first = attend(plans[0], lines, own_enc, other_enc, token_arrays, parted[0], token=token)
    last = attend(plans[1], lines, own_enc, other_enc, token_arrays, parted[1], first[:5])
    outs, own_back, other_back = last[:4], last[4], last[5]

    rows = groups * mine * piece
    (back,) = sum_blocks(
        [own_back.reshape(1, rows, width), swap_cores(other_back).reshape(1, rows, width)],
        (1,),
        to_hbm=True,
    )
    split_rows = lax.all_to_all(
        back.reshape(groups, mine, piece, width), SEQ, split_axis=0, concat_axis=0, tiled=True
    )

    count = chips // 2
    first_halves = [first[5], swap_lines(first[6], stages - 1, stages)]
    last_halves = [last[6], swap_lines(last[7], stages - 1, stages)]
    after = [in_hbm(back)]
    for stage in reversed(range(stages)):
        size = first_halves[0].size // (part_rows * 2 * columns)
        sizes = (size // 2, size // 2) if stage else (1,) * count
        flat = lambda halves: [value.reshape(size, part_rows, 2 * columns) for value in halves]
        first_flat, last_flat = flat(first_halves), flat(last_halves)
        if stage == stages - 1:
            first_flat[0], last_flat[0] = in_hbm(first_flat[0]), in_hbm(last_flat[0])
        first_sums = sum_blocks(first_flat, sizes, after)
        last_sums = sum_blocks(last_flat, sizes, [first_sums[0]])
        after = [last_sums[0]]
        if stage:
            first_halves = [first_sums[0], swap_lines(first_sums[1], stage - 1, stages)]
            last_halves = [last_sums[0], swap_lines(last_sums[1], stage - 1, stages)]
    terms = {0: first_sums[0]}
    terms |= {shift: swap_chips(value, shift) for value, shift in zip(first_sums[1:], even)}
    terms |= {shift: swap_chips(value, shift) for value, shift in zip(last_sums, odd)}
    placed = encode_back(
        slots,
        split_rows.reshape(groups * mine, piece, width),
        used,
        slope,
        gain,
        enc_up,
        enc_down,
        groups * holding,
        [terms[shift] for shift in even],
    )
    (share,) = sum_blocks([*terms.values()], (1,), [in_hbm(placed)])
    share = share[0]
    if lax.axis_size("far") > 1:
        share = lax.psum(share, "far")
    weight_grads = join_grads(part_lines, gather_lines(share, stages))

    returned = lax.all_to_all(
        placed.reshape(groups, holding, piece, width), SEQ, split_axis=0, concat_axis=0, tiled=True
    )
    pool_grad = returned.transpose(1, 0, 2, 3).reshape(1, holding, span, width)

    is_own = (lax.broadcasted_iota(jnp.int32, (1, all_columns), 1) // columns) % 2 == core
    outs = [jnp.where(is_own, outs[i], swap_cores(outs[2 + i]))[None] for i in range(2)]
    return outs[0], outs[1], pool_grad, weight_grads[0], weight_grads[1]


def solution(mesh):
    dp, seq = mesh.shape["dp"], mesh.shape["seq"]
    lines = 4 if dp % 4 == 0 else dp
    fine = Mesh(
        mesh.devices.reshape(dp // lines, lines, seq // 2, 2), ("far", "line", "z", "core")
    )
    dp_axes = ("far", "line")
    return jax.shard_map(
        on_device,
        mesh=fine,
        in_specs=(
            P(dp_axes, SEQ, None),
            P(dp_axes, SEQ, None),
            P(dp_axes, SEQ, None, None),
            P(dp_axes, None),
            P(),
            P(),
            P(),
            P(None, SEQ),
            P(None, SEQ),
        ),
        out_specs=(
            P(dp_axes, SEQ, None),
            P(dp_axes, SEQ, None),
            P(dp_axes, SEQ, None, None),
            P(None, SEQ),
            P(None, SEQ),
        ),
        check_vma=False,
    )
```
